512 devices in a mesh: nodes: 128 (over z, y, core), grp: 4 (over x).
Axes of the slice: x: 4, y: 8, z: 8, core: 2. Of those that a mesh axis runs over, the one named last changes fastest.
Arguments:
- grad_out: bfloat16 [393216, 128], P(('nodes', 'grp')), may hold values from -6 to 6
- agg_saved: bfloat16 [393216, 128], P(('nodes', 'grp')), may hold values from -6 to 6
- hidden_saved: bfloat16 [393216, 256], P(('nodes', 'grp')), may hold values from 0 to 6
- w_one: bfloat16 [128, 256], replicated, may hold values from -0.5 to 0.5
- w_two: bfloat16 [256, 128], replicated, may hold values from -0.375 to 0.375
- local_lists: int32 [393216, 16], P(('nodes', 'grp')), may hold values from 0 to 768
- send_slots: int32 [128, 4, 128, 4, 8], P('nodes', 'grp'), may hold values from 0 to 768, as said below
- receive_slots: int32 [128, 4, 128, 4, 8], P('nodes', 'grp'), may hold values from 0 to 768, as said below
Outputs:
- grad_x: bfloat16 [393216, 128], P(('nodes', 'grp'))
- grad_w1: float32 [128, 256], replicated
- grad_b1: float32 [256], replicated
- grad_w2: float32 [256, 128], replicated
- grad_b2: float32 [128], replicated
- grad_vn: float32 [128], replicated
The draws below stay inside these ranges and needn't reach their ends.
Inputs may be any that keep to these rules, and one draw needn't show every extreme that they name: For each sender and receiver the filled slots of send_slots and receive_slots are the same ones; some receivers get all 8 slots filled from every sender. `receive_slots`: filled exactly where send_slots is filled for the same pair of devices.
All inputs are finite; a program needn't handle non-finite values.
Results may differ from the reference program's by a relative error of at most 0.007.
Values may be sent and summed in bfloat16 or wider, within the bound.
No kernel may reach another device: no remote copies, remote signals or barrier semaphores. Data moves between devices by JAX's collectives and lax.ppermute only.
A program may use at most 64 MiB of HBM per device.

```python
import jax
import jax.numpy as jnp
from jax import lax

D = 128
H = 256
ROWS_DEV = 768
CAP = 8
KL = 16
TOTAL_ROWS = 393216
N_NODES = 128
N_GRP = 4
DEVICES = 512


def slot_tables(key):
    order_key = jax.random.fold_in(key, 11)
    count_key = jax.random.fold_in(key, 12)
    source_key = jax.random.fold_in(key, 13)
    target_key = jax.random.fold_in(key, 14)
    order = jax.random.permutation(order_key, DEVICES)
    is_busy = order < max(1, DEVICES // 32)
    base = jax.random.randint(count_key, (DEVICES, DEVICES), 1, CAP // 2 + 1)
    counts = jnp.where(is_busy[None, :], CAP, base)
    slot_index = jnp.arange(CAP, dtype=jnp.int32)
    filled = slot_index[None, None, :] < counts[:, :, None]
    source_rows = jax.random.randint(source_key, (DEVICES, DEVICES, CAP), 0, ROWS_DEV)
    target_rows = jax.random.randint(target_key, (DEVICES, DEVICES, CAP), 0, ROWS_DEV)
    sending = jnp.where(filled, source_rows, ROWS_DEV).astype(jnp.int32)
    receiving = jnp.transpose(jnp.where(filled, target_rows, ROWS_DEV), (1, 0, 2)).astype(jnp.int32)
    shape = (N_NODES, N_GRP, N_NODES, N_GRP, CAP)
    return (sending.reshape(shape), receiving.reshape(shape))


def draw_send_slots(key, part):
    tables = slot_tables(key)
    return tables[0]


def draw_receive_slots(key, part):
    tables = slot_tables(key)
    return tables[1]


def draw_local_lists(key, part):
    key = jax.random.fold_in(key, 5)
    count_key = jax.random.fold_in(key, 1)
    row_key = jax.random.fold_in(key, 2)
    counts = jax.random.randint(count_key, (TOTAL_ROWS, 1), KL // 4, KL + 1)
    rows_drawn = jax.random.randint(row_key, (TOTAL_ROWS, KL), 0, ROWS_DEV)
    column = jnp.arange(KL, dtype=jnp.int32)[None, :]
    return jnp.where(column < counts, rows_drawn, ROWS_DEV).astype(jnp.int32)


def draw_hidden_saved(key, part):
    key = jax.random.fold_in(key, 7)
    value_key = jax.random.fold_in(key, 1)
    values = jax.random.normal(value_key, (TOTAL_ROWS, H), jnp.float32)
    return jnp.clip(values, 0.0, 6.0).astype(jnp.bfloat16)


def shard_levels(own_key, extent, shards, low, largest):
    def one(dim, parts):
        draws = jax.random.uniform(jax.random.fold_in(jax.random.fold_in(own_key, 6), dim), (parts,), jnp.float32, low / len(shards), largest / len(shards))
        return jnp.repeat(jnp.exp(draws), extent[dim] // parts).reshape((-1,) + (1,) * (len(extent) - dim - 1))

    factor_of = one(*shards[0])
    for cut in shards[1:]:
        factor_of = factor_of * one(*cut)
    return factor_of


def gaussian(stream_key, dims, width, limit, shards=(), held_as=jnp.bfloat16):
    gain = shard_levels(stream_key, dims, shards, -0.22, 0.18) if shards else 1.0
    drawn = jax.random.normal(stream_key, dims, jnp.float32) * width * gain
    return jnp.minimum(jnp.maximum(drawn, -limit), limit).astype(held_as)


def setup_inputs(seed: int = 0) -> dict:
    splits = jax.random.split(jax.random.key(seed), 9)
    grad_out = gaussian(splits[0], (TOTAL_ROWS, D), 1.0, 6.0, ((0, 512),))
    agg_saved = gaussian(splits[1], (TOTAL_ROWS, D), 1.0, 6.0, ((0, 512),))
    hidden_saved = draw_hidden_saved(jax.random.fold_in(splits[8], 71), 0)
    w_one = gaussian(splits[3], (D, H), D ** -0.5, 0.5)
    w_two = gaussian(splits[4], (H, D), H ** -0.5, 0.375)
    local_lists = draw_local_lists(jax.random.fold_in(splits[8], 71), 0)
    send_slots = draw_send_slots(jax.random.fold_in(splits[8], 71), 0)
    receive_slots = draw_receive_slots(jax.random.fold_in(splits[8], 71), 0)
    return {"grad_out": grad_out, "agg_saved": agg_saved, "hidden_saved": hidden_saved, "w_one": w_one, "w_two": w_two, "local_lists": local_lists, "send_slots": send_slots, "receive_slots": receive_slots}


def backward_rows(pieces, w_one, w_two):
    upstream, agg_rows, hidden_rows = pieces
    grad_hidden = jnp.dot(upstream, w_two.T, preferred_element_type=jnp.float32)
    grad_z = jnp.where(hidden_rows > 0, grad_hidden, jnp.zeros_like(grad_hidden)).astype(jnp.bfloat16)
    grad_agg = jnp.dot(grad_z, w_one.T, preferred_element_type=jnp.float32)
    part_w2 = jnp.dot(hidden_rows.T, upstream, preferred_element_type=jnp.float32)
    part_b2 = jnp.sum(upstream.astype(jnp.float32), axis=0)
    part_w1 = jnp.dot(agg_rows.T, grad_z, preferred_element_type=jnp.float32)
    part_b1 = jnp.sum(grad_z.astype(jnp.float32), axis=0)
    return grad_agg, part_w1, part_b1, part_w2, part_b2


def reference(grad_out, agg_saved, hidden_saved, w_one, w_two, local_lists, send_slots, receive_slots):
    upstream = grad_out.reshape(DEVICES, ROWS_DEV, D)
    agg_rows = agg_saved.reshape(DEVICES, ROWS_DEV, D)
    hidden_rows = hidden_saved.reshape(DEVICES, ROWS_DEV, H)
    grad_agg, part_w1, part_b1, part_w2, part_b2 = lax.map(
        lambda pieces: backward_rows(pieces, w_one, w_two), (upstream, agg_rows, hidden_rows))
    agg_wire = grad_agg.astype(jnp.bfloat16)
    padded = jnp.concatenate([agg_wire, jnp.zeros((DEVICES, 1, D), jnp.bfloat16)], axis=1)
    sender_table = jnp.transpose(send_slots.reshape(DEVICES, DEVICES, CAP), (1, 0, 2))
    target_table = receive_slots.reshape(DEVICES, DEVICES, CAP)
    local_table = local_lists.reshape(DEVICES, ROWS_DEV, KL)
    senders = jnp.arange(DEVICES, dtype=jnp.int32)[:, None]

    def finish(pieces):
        sender_rows, targets, own_agg, own_padded, own_lists = pieces
        arrived = padded[senders, sender_rows].reshape(DEVICES * CAP, D).astype(jnp.float32)
        remote = jnp.zeros((ROWS_DEV + 1, D), jnp.float32).at[targets.reshape(-1)].add(arrived)[:ROWS_DEV]
        local = jnp.sum(own_padded[own_lists].astype(jnp.float32), axis=1)
        total = own_agg + local + remote
        return total.astype(jnp.bfloat16), jnp.sum(total, axis=0)

    grad_rows, node_parts = lax.map(finish, (sender_table, target_table, grad_agg, padded, local_table))
    scale = 1.0 / DEVICES
    return (grad_rows.reshape(TOTAL_ROWS, D),
            jnp.sum(part_w1, axis=0) * scale,
            jnp.sum(part_b1, axis=0) * scale,
            jnp.sum(part_w2, axis=0) * scale,
            jnp.sum(part_b2, axis=0) * scale,
            jnp.sum(node_parts, axis=0) * scale)
```

```python
import functools

import jax
import jax.numpy as jnp
from jax import lax
from jax.experimental import pallas as pl
from jax.experimental.pallas import tpu as pltpu
from jax.sharding import PartitionSpec as P

BF16 = jnp.bfloat16
F32 = jnp.float32
PLAIN = (((1,), (0,)), ((), ()))
LAST = (((1,), (1,)), ((), ()))
FIRST = (((0,), (0,)), ((), ()))
LANES = 128
EXTRA = 2
AXES = ("nodes", "grp")


def dot(a, b, dims=PLAIN):
    return lax.dot_general(a, b, dims, preferred_element_type=F32)


def iota(shape, dim):
    return lax.broadcasted_iota(jnp.int32, shape, dim)


def code(index):
    return ((LANES + (index & (LANES - 1))) << (index >> 7)).astype(F32)


def match(a, b):
    return jnp.where(a == b, 1.0, 0.0).astype(BF16)


def low_part(value):
    return value - value.astype(BF16).astype(F32)


def columns(row):
    return jnp.broadcast_to(row, (LANES, LANES)).T


def remainders(wide, thin):
    lane = iota(wide.shape, 1)
    low = jnp.where(lane == LANES - 2, thin, low_part(wide))
    return jnp.where(lane == LANES - 1, low_part(thin), low).astype(BF16)


def first_kernel(
    send_ref, lists_ref, out_ref, hid_ref, saved_ref, w1_ref, w2_ref,
    piece_ref, total_ref,
    wire_ref, counts_ref, high_ref, low_ref, wide_ref, sent_ref, place_ref, chosen_ref, mail_ref, node_ref,
):
    groups, slots, nodes = send_ref.shape
    rows = out_ref.shape[0]
    piece = slots + EXTRA
    out = out_ref[...]
    hidden = hid_ref[...]
    grad_hidden = dot(out, w2_ref[...], LAST)
    grad_z = jnp.where(hidden > 0, grad_hidden, 0.0).astype(BF16)
    grad_agg = dot(grad_z, w1_ref[...], LAST)
    wire_ref[...] = grad_agg.astype(BF16)

    row_code = code(iota((rows, LANES), 0)).astype(BF16)
    for tile in range(rows // LANES):
        lists = code(lists_ref[:, tile * LANES : (tile + 1) * LANES]).astype(BF16)
        counts = match(lists[0:1], row_code)
        for k in range(1, lists_ref.shape[0]):
            counts += match(lists[k : k + 1], row_code)
        counts_ref[:, tile * LANES : (tile + 1) * LANES] = counts
    local = dot(wire_ref[...].T, counts_ref[...])
    total = grad_agg + local.T
    total_ref[...] = total
    node_ref[...] = jnp.sum(total, axis=0, keepdims=True)

    part_w1 = dot(saved_ref[...], grad_z, FIRST)
    part_w2 = dot(out, hidden, FIRST)
    sum_z = jnp.sum(grad_z.astype(F32), axis=0, keepdims=True)
    sum_out = jnp.sum(out.astype(F32), axis=0, keepdims=True)
    quarters = [
        (part_w1[:, :LANES], sum_z[:, :LANES]),
        (part_w1[:, LANES:], sum_z[:, LANES:]),
        (part_w2[:, :LANES], sum_out),
    ]
    for q, (wide, thin) in enumerate(quarters):
        high_ref[q * LANES : (q + 1) * LANES, :] = wide.astype(BF16)
        low_ref[q * LANES : (q + 1) * LANES, :] = remainders(wide, columns(thin))
    wide_ref[...] = part_w2[:, LANES:]
    high_ref[3 * LANES :, :] = part_w2[:, LANES:].astype(BF16)

    parts = []
    for g in range(groups):
        parts += [code(send_ref[g]), jnp.zeros((EXTRA, nodes), F32)]
    sent = jnp.concatenate(parts, axis=0)
    sent_ref[...] = jnp.concatenate([sent, pltpu.roll(sent, nodes - 1, 1)], axis=0)
    lane = iota(place_ref.shape, 1)
    place_ref[...] = match(
        iota(place_ref.shape, 0), piece * (lane & (LANES - 1)) + slots + (lane >> 7)
    )
    lane_code = code(iota((16, rows), 1)).astype(BF16)
    block = LANES * piece
    width = LANES // groups
    steps = nodes // width

    @pl.loop(0, steps)
    def _(step):
        sent = pltpu.roll(sent_ref[...], nodes - step * width, 1).astype(BF16)
        for n in range(0, width, 2):
            for r in range(0, 2 * groups * piece, 16):
                column = jnp.broadcast_to(sent[r : r + 16, n : n + 1], (16, rows))
                chosen_ref[n * groups * piece + r : n * groups * piece + r + 16, :] = match(column, lane_code)
        mail = dot(chosen_ref[...], wire_ref[...])
        mail_ref[...] = mail
        node_ref[...] += jnp.sum(mail, axis=0, keepdims=True)

        @pl.when(step == steps - 1)
        def _():
            low_ref[3 * LANES :, :] = remainders(wide_ref[...], columns(node_ref[...]))

        own = pl.ds(pl.multiple_of(step * LANES, LANES), LANES)
        sums = jnp.concatenate([high_ref[own, :], low_ref[own, :]], axis=0)
        piece_ref[pl.ds(pl.multiple_of(step * block, block), block), :] = (
            mail_ref[...] + dot(place_ref[...], sums)
        ).astype(BF16)


def chunk_kernel(piece, scale, arrived_ref, share_ref):
    span = piece * LANES
    lane = iota((16, span), 1)
    place = lane - piece * ((lane * ((1 << 16) // piece + 1)) >> 16)
    pick = match(place, piece - EXTRA + iota((16, span), 0))
    sums = jnp.zeros((16, LANES), F32)
    for start in range(0, arrived_ref.shape[0], span):
        sums += dot(pick, arrived_ref[start : start + span, :])
    high, low = sums[0:1], sums[1:2]
    lane = iota(high.shape, 1)
    last = jnp.sum(jnp.where(lane >= LANES - 2, low, 0.0), axis=1, keepdims=True)
    wide = scale * (high + jnp.where(lane >= LANES - 2, 0.0, low))
    thin = jnp.broadcast_to(scale * last, wide.shape)
    pair = jnp.concatenate([wide.astype(BF16), remainders(wide, thin)], axis=0)
    share_ref[...] = jnp.concatenate([pair] * (share_ref.shape[0] // EXTRA), axis=0)


def remote_kernel(recv_ref, arrived_ref, total_ref, x_ref):
    rows = total_ref.shape[0]
    row_code = code(iota((rows, LANES), 0)).astype(BF16)
    targets = code(recv_ref[...]).astype(BF16)
    total = total_ref[...]
    for r in range(0, recv_ref.shape[0], 2):
        chosen = jnp.concatenate([match(targets[q : q + 1], row_code) for q in (r, r + 1)], axis=1)
        total += dot(chosen, arrived_ref[r * LANES : (r + 2) * LANES, :])
    x_ref[...] = total.astype(BF16)


def last_kernel(share_ref, w1_ref, b1_ref, w2_ref, b2_ref, node_ref, rows_ref):
    rows_ref[...] = share_ref[...].astype(F32)
    half = rows_ref.shape[0] // 2
    high = rows_ref[pl.ds(0, half, 2), :]
    low = rows_ref[pl.ds(1, half, 2), :]
    lane = iota(high.shape, 1)
    wide = high + jnp.where(lane >= LANES - 2, 0.0, low)
    w1_ref[:, :LANES] = wide[:LANES]
    w1_ref[:, LANES:] = wide[LANES : 2 * LANES]
    w2_ref[:LANES, :] = wide[2 * LANES : 3 * LANES].T
    w2_ref[LANES:, :] = wide[3 * LANES :].T
    thin = []
    for q in range(4):
        turned = low[q * LANES : (q + 1) * LANES].T
        thin.append(turned[LANES - 2 : LANES - 1] + turned[LANES - 1 :])
    b1_ref[...] = jnp.concatenate(thin[:2], axis=1)
    b2_ref[...] = thin[2]
    node_ref[...] = thin[3]


def call(kernel, outs, scratch=(), **cost):
    return pl.pallas_call(
        kernel,
        out_shape=[jax.ShapeDtypeStruct(shape, dtype) for shape, dtype in outs],
        scratch_shapes=list(scratch),
        compiler_params=pltpu.CompilerParams(vmem_limit_bytes=24 << 20),
        cost_estimate=pl.CostEstimate(transcendentals=0, **cost),
    )


def per_device(
    grad_out, agg_saved, hidden_saved, w_one, w_two, local_lists, send_slots, receive_slots
):
    rows, width = grad_out.shape
    hidden = hidden_saved.shape[1]
    nodes, groups, slots = send_slots.shape[2:]
    devices = nodes * groups
    piece = slots + EXTRA
    send = jnp.transpose(send_slots[0, 0], (1, 2, 0))
    pieces, total = call(
        first_kernel,
        [((devices * piece, width), BF16), ((rows, width), F32)],
        [
            pltpu.VMEM((rows, width), BF16),
            pltpu.VMEM((rows, rows), BF16),
            pltpu.VMEM((devices, LANES), BF16),
            pltpu.VMEM((devices, LANES), BF16),
            pltpu.VMEM((LANES, LANES), F32),
            pltpu.VMEM((2 * groups * piece, nodes), F32),
            pltpu.VMEM((LANES * piece, 2 * LANES), BF16),
            pltpu.VMEM((LANES * piece, rows), BF16),
            pltpu.VMEM((LANES * piece, width), F32),
            pltpu.VMEM((1, width), F32),
        ],
        flops=2 * (devices * piece + rows) * rows * width,
        bytes_accessed=devices * piece * width * 2,
    )(send, local_lists.T, grad_out, hidden_saved, agg_saved, w_one, w_two)

    def exchange(x, height):
        x = x.reshape(devices, height // 2, 2, width)
        return lax.all_to_all(x, AXES, split_axis=0, concat_axis=0, tiled=True).reshape(-1, width)

    arrived = exchange(pieces, piece)
    (share,) = call(
        functools.partial(chunk_kernel, piece, 1.0 / devices),
        [((devices * EXTRA, width), BF16)],
        flops=2 * 16 * devices * piece * width,
        bytes_accessed=devices * piece * width * 2,
    )(arrived)
    shares = exchange(share, EXTRA)
    recv = jnp.pad(receive_slots[0, 0], ((0, 0), (0, 0), (0, EXTRA)), constant_values=rows)
    (grad_x,) = call(
        remote_kernel,
        [((rows, width), BF16)],
        flops=2 * devices * piece * rows * width,
        bytes_accessed=devices * piece * width * 2,
    )(recv.reshape(-1, LANES), arrived, total)
    w1, b1, w2, b2, node = call(
        last_kernel,
        [
            ((width, hidden), F32),
            ((1, hidden), F32),
            ((hidden, width), F32),
            ((1, width), F32),
            ((1, width), F32),
        ],
        [pltpu.VMEM((devices * EXTRA, width), F32)],
        flops=0,
        bytes_accessed=devices * EXTRA * width * 2,
    )(shares)
    return grad_x, w1, b1[0], w2, b2[0], node[0]


def solution(mesh):
    placed = (
        P(AXES, None),
        P(AXES, None),
        P(AXES, None),
        P(),
        P(),
        P(AXES, None),
        P("nodes", "grp", None, None, None),
        P("nodes", "grp", None, None, None),
    )
    return jax.shard_map(
        per_device,
        mesh=mesh,
        in_specs=placed,
        out_specs=(P(AXES, None), P(), P(), P(), P(), P()),
        check_vma=False,
    )
```

```python
import functools

import jax
import jax.numpy as jnp
from jax import lax
from jax.experimental import pallas as pl
from jax.experimental.pallas import tpu as pltpu
from jax.sharding import PartitionSpec as P

BF16 = jnp.bfloat16
F32 = jnp.float32
PLAIN = (((1,), (0,)), ((), ()))
LAST = (((1,), (1,)), ((), ()))
FIRST = (((0,), (0,)), ((), ()))
LANES = 128
EXTRA = 2
AXES = ("nodes", "grp")


def dot(a, b, dims=PLAIN):
    return lax.dot_general(a, b, dims, preferred_element_type=F32)


def iota(shape, dim):
    return lax.broadcasted_iota(jnp.int32, shape, dim)


def match(a, b):
    shape = jnp.broadcast_shapes(a.shape, b.shape)
    return jnp.where(a == b, jnp.ones(shape, BF16), jnp.zeros(shape, BF16))


def low_part(value):
    return value - value.astype(BF16).astype(F32)


def columns(row):
    return jnp.broadcast_to(row, (LANES, LANES)).T


def remainders(wide, thin):
    lane = iota(wide.shape, 1)
    low = jnp.where(lane == LANES - 2, thin, low_part(wide))
    return jnp.where(lane == LANES - 1, low_part(thin), low).astype(BF16)


def first_kernel(
    send_hbm, lists_hbm, out_hbm, hid_hbm, saved_hbm, w1_hbm, w2_hbm,
    piece_ref, agg_ref, wire_ref,
    send_ref, lists_ref, out_ref, hid_ref, saved_ref, w1_ref, w2_ref, sems,
    high_ref, low_ref, sent_ref, rows_ref, chosen_ref,
):
    groups, slots, nodes = send_ref.shape
    rows = out_ref.shape[0]
    piece = slots + EXTRA
    pairs = [
        (out_hbm, out_ref), (w2_hbm, w2_ref), (hid_hbm, hid_ref), (w1_hbm, w1_ref),
        (saved_hbm, saved_ref), (lists_hbm, lists_ref), (send_hbm, send_ref),
    ]
    copies = [pltpu.make_async_copy(a, b, sems.at[i]) for i, (a, b) in enumerate(pairs)]
    for copy in copies:
        copy.start()

    block = LANES * piece
    lane = iota((block, 2 * LANES), 1)
    chosen_ref[:, rows:] = jnp.where(
        iota(lane.shape, 0) == piece * (lane & (LANES - 1)) + slots + (lane >> 7), 1.0, 0.0
    ).astype(BF16)

    for copy in copies[:4]:
        copy.wait()
    out = out_ref[...]
    hidden = hid_ref[...]
    grad_hidden = dot(out, w2_ref[...], LAST)
    grad_z = jnp.where(hidden > 0, grad_hidden, 0.0).astype(BF16)
    grad_agg = dot(grad_z, w1_ref[...], LAST)
    wire = grad_agg.astype(BF16)
    agg_ref[...] = grad_agg
    wire_ref[...] = wire
    rows_ref[:rows, :] = wire
    for copy in copies[4:]:
        copy.wait()

    low_row = iota((LANES, 1), 0).astype(jnp.int16)
    high_row = iota((16, 1), 0).astype(jnp.int16)
    count = jnp.zeros((LANES, 16), F32)
    for ref in [lists_ref] + [send_ref.at[g] for g in range(groups)]:
        index = ref[...]
        low = (index & (LANES - 1)).astype(jnp.int16)
        high = (index >> 7).astype(jnp.int16)
        for k in range(index.shape[0]):
            count += dot(match(low[k : k + 1], low_row), match(high[k : k + 1], high_row), LAST)
    node = jnp.sum(grad_agg, axis=0, keepdims=True)
    for h in range(rows // LANES):
        carried = wire[h * LANES : (h + 1) * LANES].astype(F32) * count[:, h : h + 1]
        node += jnp.sum(carried, axis=0, keepdims=True)

    part_w1 = dot(saved_ref[...], grad_z, FIRST)
    part_w2 = dot(out, hidden, FIRST)
    sum_z = jnp.sum(grad_z.astype(F32), axis=0, keepdims=True)
    sum_out = jnp.sum(out.astype(F32), axis=0, keepdims=True)
    quarters = [
        (part_w1[:, :LANES], sum_z[:, :LANES]),
        (part_w1[:, LANES:], sum_z[:, LANES:]),
        (part_w2[:, :LANES], sum_out),
        (part_w2[:, LANES:], node),
    ]
    for q, (wide, thin) in enumerate(quarters):
        high_ref[q * LANES : (q + 1) * LANES, :] = wide.astype(BF16)
        low_ref[q * LANES : (q + 1) * LANES, :] = remainders(wide, columns(thin))

    parts = []
    for g in range(groups):
        parts += [send_ref[g], jnp.full((EXTRA, nodes), rows, jnp.int32)]
    sent = jnp.concatenate(parts, axis=0)
    sent_ref[...] = jnp.concatenate([sent, pltpu.roll(sent, nodes - 1, 1)], axis=0)
    lane_index = iota((16, rows), 1).astype(jnp.int16)
    width = LANES // groups

    @pl.loop(0, nodes // width)
    def _(step):
        own = pl.ds(pl.multiple_of(step * LANES, LANES), LANES)
        rows_ref[rows : rows + LANES, :] = high_ref[own, :]
        rows_ref[rows + LANES :, :] = low_ref[own, :]
        sent = pltpu.roll(sent_ref[...], nodes - step * width, 1).astype(jnp.int16)
        for n in range(0, width, 2):
            for r in range(0, 2 * groups * piece, 16):
                column = jnp.broadcast_to(sent[r : r + 16, n : n + 1], (16, rows))
                start = n * groups * piece + r
                chosen_ref[start : start + 16, :rows] = match(column, lane_index)
        piece_ref[pl.ds(pl.multiple_of(step * block, block), block), :] = dot(
            chosen_ref[...], rows_ref[...]
        ).astype(BF16)


def local_kernel(lists_ref, recv_ref, wire_ref, agg_ref, total_ref, target_ref, counts_ref):
    rows = wire_ref.shape[0]
    row_index = iota((rows, 1), 0).astype(jnp.int16)
    for tile in range(rows // LANES):
        lists = lists_ref[:, tile * LANES : (tile + 1) * LANES].astype(jnp.int16)
        counts = match(lists[0:1], row_index)
        for k in range(1, lists_ref.shape[0]):
            counts += match(lists[k : k + 1], row_index)
        counts_ref[:, tile * LANES : (tile + 1) * LANES] = counts
    local = dot(wire_ref[...].T, counts_ref[...])
    total_ref[...] = agg_ref[...] + local.T
    target_ref[...] = recv_ref[...]


def chunk_kernel(piece, scale, arrived_ref, share_ref):
    span = piece * LANES
    lane = iota((16, span), 1)
    place = lane - piece * ((lane * ((1 << 16) // piece + 1)) >> 16)
    pick = jnp.where(place == piece - EXTRA + iota((16, span), 0), 1.0, 0.0).astype(BF16)
    sums = jnp.zeros((16, LANES), F32)
    for start in range(0, arrived_ref.shape[0], span):
        sums += dot(pick, arrived_ref[start : start + span, :])
    high, low = sums[0:1], sums[1:2]
    lane = iota(high.shape, 1)
    last = jnp.sum(jnp.where(lane >= LANES - 2, low, 0.0), axis=1, keepdims=True)
    wide = scale * (high + jnp.where(lane >= LANES - 2, 0.0, low))
    thin = jnp.broadcast_to(scale * last, wide.shape)
    pair = jnp.concatenate([wide.astype(BF16), remainders(wide, thin)], axis=0)
    share_ref[...] = jnp.concatenate([pair] * (share_ref.shape[0] // EXTRA), axis=0)


def remote_kernel(recv_ref, arrived_ref, total_ref, x_ref):
    rows = total_ref.shape[0]
    row_index = iota((rows, 1), 0).astype(jnp.int16)
    targets = recv_ref[...].astype(jnp.int16)
    total = total_ref[...]
    for r in range(0, recv_ref.shape[0], 2):
        chosen = jnp.concatenate([match(targets[q : q + 1], row_index) for q in (r, r + 1)], axis=1)
        total += dot(chosen, arrived_ref[r * LANES : (r + 2) * LANES, :])
    x_ref[...] = total.astype(BF16)


def last_kernel(share_ref, w1_ref, b1_ref, w2_ref, b2_ref, node_ref, rows_ref):
    rows_ref[...] = share_ref[...].astype(F32)
    half = rows_ref.shape[0] // 2
    high = rows_ref[pl.ds(0, half, 2), :]
    low = rows_ref[pl.ds(1, half, 2), :]
    lane = iota(high.shape, 1)
    wide = high + jnp.where(lane >= LANES - 2, 0.0, low)
    w1_ref[:, :LANES] = wide[:LANES]
    w1_ref[:, LANES:] = wide[LANES : 2 * LANES]
    w2_ref[:LANES, :] = wide[2 * LANES : 3 * LANES].T
    w2_ref[LANES:, :] = wide[3 * LANES :].T
    thin = []
    for q in range(4):
        turned = low[q * LANES : (q + 1) * LANES].T
        thin.append(turned[LANES - 2 : LANES - 1] + turned[LANES - 1 :])
    b1_ref[...] = jnp.concatenate(thin[:2], axis=1)
    b2_ref[...] = thin[2]
    node_ref[...] = thin[3]


def call(kernel, outs, scratch=(), hbm=0, limit=24, **cost):
    specs = {"in_specs": [pl.BlockSpec(memory_space=pltpu.HBM)] * hbm} if hbm else {}
    return pl.pallas_call(
        kernel,
        out_shape=[jax.ShapeDtypeStruct(shape, dtype) for shape, dtype in outs],
        scratch_shapes=list(scratch),
        compiler_params=pltpu.CompilerParams(vmem_limit_bytes=limit << 20),
        cost_estimate=pl.CostEstimate(transcendentals=0, **cost),
        **specs,
    )


def per_device(
    grad_out, agg_saved, hidden_saved, w_one, w_two, local_lists, send_slots, receive_slots
):
    rows, width = grad_out.shape
    hidden = hidden_saved.shape[1]
    nodes, groups, slots = send_slots.shape[2:]
    devices = nodes * groups
    piece = slots + EXTRA
    lists = local_lists.T
    sources = [jnp.transpose(send_slots[0, 0], (1, 2, 0)), lists, grad_out, hidden_saved, agg_saved, w_one, w_two]
    pieces, agg, wire = call(
        first_kernel,
        [((devices * piece, width), BF16), ((rows, width), F32), ((rows, width), BF16)],
        [pltpu.VMEM(x.shape, x.dtype) for x in sources]
        + [
            pltpu.SemaphoreType.DMA((len(sources),)),
            pltpu.VMEM((devices, LANES), BF16),
            pltpu.VMEM((devices, LANES), BF16),
            pltpu.VMEM((2 * groups * piece, nodes), jnp.int32),
            pltpu.VMEM((rows + 2 * LANES, width), BF16),
            pltpu.VMEM((LANES * piece, rows + 2 * LANES), BF16),
        ],
        hbm=len(sources),
        limit=60,
        flops=2 * devices * piece * rows * width,
        bytes_accessed=devices * piece * width * 2,
    )(*sources)
    recv = jnp.pad(receive_slots[0, 0], ((0, 0), (0, 0), (0, EXTRA)), constant_values=rows)
    total, targets = call(
        local_kernel,
        [((rows, width), F32), ((devices * piece // LANES, LANES), jnp.int32)],
        [pltpu.VMEM((rows, rows), BF16)],
        flops=2 * rows * rows * width,
        bytes_accessed=rows * width * 10,
    )(lists, recv.reshape(-1, LANES), wire, agg)

    def exchange(x, height):
        x = x.reshape(devices, height // 2, 2, width)
        return lax.all_to_all(x, AXES, split_axis=0, concat_axis=0, tiled=True).reshape(-1, width)

    arrived = exchange(pieces, piece)
    (share,) = call(
        functools.partial(chunk_kernel, piece, 1.0 / devices),
        [((devices * EXTRA, width), BF16)],
        flops=2 * 16 * devices * piece * width,
        bytes_accessed=devices * piece * width * 2,
    )(arrived)
    shares = exchange(share, EXTRA)
    (grad_x,) = call(
        remote_kernel,
        [((rows, width), BF16)],
        flops=2 * devices * piece * rows * width,
        bytes_accessed=devices * piece * width * 2,
    )(targets, arrived, total)
    w1, b1, w2, b2, node = call(
        last_kernel,
        [
            ((width, hidden), F32),
            ((1, hidden), F32),
            ((hidden, width), F32),
            ((1, width), F32),
            ((1, width), F32),
        ],
        [pltpu.VMEM((devices * EXTRA, width), F32)],
        flops=0,
        bytes_accessed=devices * EXTRA * width * 2,
    )(shares)
    return grad_x, w1, b1[0], w2, b2[0], node[0]


def solution(mesh):
    placed = (
        P(AXES, None),
        P(AXES, None),
        P(AXES, None),
        P(),
        P(),
        P(AXES, None),
        P("nodes", "grp", None, None, None),
        P("nodes", "grp", None, None, None),
    )
    return jax.shard_map(
        per_device,
        mesh=mesh,
        in_specs=placed,
        out_specs=(P(AXES, None), P(), P(), P(), P(), P()),
        check_vma=False,
    )
```

```python
import functools

import jax
import jax.numpy as jnp
from jax import lax
from jax.experimental import pallas as pl
from jax.experimental.pallas import tpu as pltpu
from jax.sharding import PartitionSpec as P

BF16 = jnp.bfloat16
F32 = jnp.float32
PLAIN = (((1,), (0,)), ((), ()))
LAST = (((1,), (1,)), ((), ()))
FIRST = (((0,), (0,)), ((), ()))
LANES = 128
EXTRA = 2
AXES = ("nodes", "grp")


def dot(a, b, dims=PLAIN):
    return lax.dot_general(a, b, dims, preferred_element_type=F32)


def iota(shape, dim):
    return lax.broadcasted_iota(jnp.int32, shape, dim)


def match(a, b):
    shape = jnp.broadcast_shapes(a.shape, b.shape)
    return jnp.where(a == b, jnp.ones(shape, BF16), jnp.zeros(shape, BF16))


def low_part(value):
    return value - value.astype(BF16).astype(F32)


def columns(row):
    return jnp.broadcast_to(row, (LANES, LANES)).T


def remainders(wide, thin):
    lane = iota(wide.shape, 1)
    low = jnp.where(lane == LANES - 2, thin, low_part(wide))
    return jnp.where(lane == LANES - 1, low_part(thin), low).astype(BF16)


def first_kernel(
    send_hbm, out_hbm, w2_hbm, hid_hbm, w1_hbm, lists_hbm, saved_hbm,
    piece_hbm, agg_hbm, wire_hbm,
    send_ref, out_ref, w2_ref, hid_ref, w1_ref, lists_ref, saved_ref, in_sems,
    piece_ref, agg_ref, wire_ref, out_sems,
    rows_ref, chosen_ref,
):
    groups, slots, nodes = send_ref.shape
    rows = out_ref.shape[0]
    piece = slots + EXTRA
    block = LANES * piece
    width = LANES // groups
    blocks = nodes // width
    pairs = [
        (send_hbm, send_ref), (out_hbm, out_ref), (w2_hbm, w2_ref), (hid_hbm, hid_ref),
        (w1_hbm, w1_ref), (lists_hbm, lists_ref), (saved_hbm, saved_ref),
    ]
    arrivals = [pltpu.make_async_copy(a, b, in_sems.at[i]) for i, (a, b) in enumerate(pairs)]
    for copy in arrivals:
        copy.start()

    lane = iota((block, 2 * LANES), 1)
    place = jnp.where(
        iota(lane.shape, 0) == piece * (lane & (LANES - 1)) + slots + (lane >> 7), 1.0, 0.0
    ).astype(BF16)
    for step in range(blocks):
        chosen_ref[step, :, rows:] = place

    arrivals[0].wait()
    parts = []
    for g in range(groups):
        parts += [send_ref[g], jnp.full((EXTRA, nodes), rows, jnp.int32)]
    sent = jnp.concatenate(parts, axis=0)
    sent = jnp.concatenate([sent, pltpu.roll(sent, nodes - 1, 1)], axis=0).astype(jnp.int16)
    lane_index = iota((16, rows), 1).astype(jnp.int16)

    def choose(step):
        for n in range(0, width, 2):
            for r in range(0, 2 * groups * piece, 16):
                at = step * width + n
                column = jnp.broadcast_to(sent[r : r + 16, at : at + 1], (16, rows))
                start = n * groups * piece + r
                chosen_ref[step, start : start + 16, :rows] = match(column, lane_index)

    choose(0)
    for copy in arrivals[1:5]:
        copy.wait()
    out = out_ref[...]
    hidden = hid_ref[...]
    grad_hidden = dot(out, w2_ref[...], LAST)
    grad_z = jnp.where(hidden > 0, grad_hidden, 0.0).astype(BF16)
    grad_agg = dot(grad_z, w1_ref[...], LAST)
    wire = grad_agg.astype(BF16)
    agg_ref[...] = grad_agg
    wire_ref[...] = wire
    departures = [
        pltpu.make_async_copy(agg_ref, agg_hbm, out_sems.at[0]),
        pltpu.make_async_copy(wire_ref, wire_hbm, out_sems.at[1]),
    ]
    for copy in departures:
        copy.start()
    for step in range(blocks):
        rows_ref[step, :rows, :] = wire
    for copy in arrivals[5:]:
        copy.wait()

    low_row = iota((LANES, 1), 0).astype(jnp.int16)
    high_row = iota((16, 1), 0).astype(jnp.int16)
    count = jnp.zeros((LANES, 16), F32)
    for ref in [lists_ref] + [send_ref.at[g] for g in range(groups)]:
        index = ref[...]
        low = (index & (LANES - 1)).astype(jnp.int16)
        high = (index >> 7).astype(jnp.int16)
        for k in range(index.shape[0]):
            count += dot(match(low[k : k + 1], low_row), match(high[k : k + 1], high_row), LAST)
    node = jnp.sum(grad_agg, axis=0, keepdims=True)
    for h in range(rows // LANES):
        carried = wire[h * LANES : (h + 1) * LANES].astype(F32) * count[:, h : h + 1]
        node += jnp.sum(carried, axis=0, keepdims=True)

    part_w1 = dot(saved_ref[...], grad_z, FIRST)
    part_w2 = dot(out, hidden, FIRST)
    sum_z = jnp.sum(grad_z.astype(F32), axis=0, keepdims=True)
    sum_out = jnp.sum(out.astype(F32), axis=0, keepdims=True)
    quarters = [
        (part_w1[:, :LANES], sum_z[:, :LANES]),
        (part_w1[:, LANES:], sum_z[:, LANES:]),
        (part_w2[:, :LANES], sum_out),
        (part_w2[:, LANES:], node),
    ]

    for step, (wide, thin) in enumerate(quarters):
        if step:
            choose(step)
        rows_ref[step, rows : rows + LANES, :] = wide.astype(BF16)
        rows_ref[step, rows + LANES :, :] = remainders(wide, columns(thin))
        own = pl.ds(step * block, block)
        piece_ref[own, :] = dot(chosen_ref[step], rows_ref[step]).astype(BF16)
        copy = pltpu.make_async_copy(piece_ref.at[own], piece_hbm.at[own], out_sems.at[2 + step])
        copy.start()
        departures.append(copy)
    for copy in departures:
        copy.wait()


def local_kernel(lists_ref, recv_ref, wire_ref, agg_ref, total_ref, target_ref, counts_ref):
    rows = wire_ref.shape[0]
    row_index = iota((rows, 1), 0).astype(jnp.int16)
    for tile in range(rows // LANES):
        lists = lists_ref[:, tile * LANES : (tile + 1) * LANES].astype(jnp.int16)
        counts = match(lists[0:1], row_index)
        for k in range(1, lists_ref.shape[0]):
            counts += match(lists[k : k + 1], row_index)
        counts_ref[:, tile * LANES : (tile + 1) * LANES] = counts
    local = dot(wire_ref[...].T, counts_ref[...])
    total_ref[...] = agg_ref[...] + local.T
    target_ref[...] = recv_ref[...]


def chunk_kernel(piece, scale, arrived_ref, share_ref):
    span = piece * LANES
    lane = iota((16, span), 1)
    place = lane - piece * ((lane * ((1 << 16) // piece + 1)) >> 16)
    pick = jnp.where(place == piece - EXTRA + iota((16, span), 0), 1.0, 0.0).astype(BF16)
    sums = jnp.zeros((16, LANES), F32)
    for start in range(0, arrived_ref.shape[0], span):
        sums += dot(pick, arrived_ref[start : start + span, :])
    high, low = sums[0:1], sums[1:2]
    lane = iota(high.shape, 1)
    last = jnp.sum(jnp.where(lane >= LANES - 2, low, 0.0), axis=1, keepdims=True)
    wide = scale * (high + jnp.where(lane >= LANES - 2, 0.0, low))
    thin = jnp.broadcast_to(scale * last, wide.shape)
    pair = jnp.concatenate([wide.astype(BF16), remainders(wide, thin)], axis=0)
    share_ref[...] = jnp.concatenate([pair] * (share_ref.shape[0] // EXTRA), axis=0)


def remote_kernel(recv_ref, arrived_ref, total_ref, x_ref):
    rows = total_ref.shape[0]
    row_index = iota((rows, 1), 0).astype(jnp.int16)
    targets = recv_ref[...].astype(jnp.int16)
    total = total_ref[...]
    for r in range(0, recv_ref.shape[0], 2):
        chosen = jnp.concatenate([match(targets[q : q + 1], row_index) for q in (r, r + 1)], axis=1)
        total += dot(chosen, arrived_ref[r * LANES : (r + 2) * LANES, :])
    x_ref[...] = total.astype(BF16)


def last_kernel(share_ref, w1_ref, b1_ref, w2_ref, b2_ref, node_ref, rows_ref):
    rows_ref[...] = share_ref[...].astype(F32)
    half = rows_ref.shape[0] // 2
    high = rows_ref[pl.ds(0, half, 2), :]
    low = rows_ref[pl.ds(1, half, 2), :]
    lane = iota(high.shape, 1)
    wide = high + jnp.where(lane >= LANES - 2, 0.0, low)
    w1_ref[:, :LANES] = wide[:LANES]
    w1_ref[:, LANES:] = wide[LANES : 2 * LANES]
    w2_ref[:LANES, :] = wide[2 * LANES : 3 * LANES].T
    w2_ref[LANES:, :] = wide[3 * LANES :].T
    thin = []
    for q in range(4):
        turned = low[q * LANES : (q + 1) * LANES].T
        thin.append(turned[LANES - 2 : LANES - 1] + turned[LANES - 1 :])
    b1_ref[...] = jnp.concatenate(thin[:2], axis=1)
    b2_ref[...] = thin[2]
    node_ref[...] = thin[3]


def call(kernel, outs, scratch=(), far=0, limit=24, **cost):
    hbm = pl.BlockSpec(memory_space=pltpu.HBM)
    specs = {"in_specs": [hbm] * far, "out_specs": [hbm] * len(outs)} if far else {}
    return pl.pallas_call(
        kernel,
        out_shape=[jax.ShapeDtypeStruct(shape, dtype) for shape, dtype in outs],
        scratch_shapes=list(scratch),
        compiler_params=pltpu.CompilerParams(vmem_limit_bytes=limit << 20),
        cost_estimate=pl.CostEstimate(transcendentals=0, **cost),
        **specs,
    )


def per_device(
    grad_out, agg_saved, hidden_saved, w_one, w_two, local_lists, send_slots, receive_slots
):
    rows, width = grad_out.shape
    hidden = hidden_saved.shape[1]
    nodes, groups, slots = send_slots.shape[2:]
    devices = nodes * groups
    piece = slots + EXTRA
    lists = local_lists.T
    send = jnp.transpose(send_slots[0, 0], (1, 2, 0))
    sources = [send, grad_out, w_two, hidden_saved, w_one, lists, agg_saved]
    outs = [((devices * piece, width), BF16), ((rows, width), F32), ((rows, width), BF16)]
    blocks = devices // LANES
    pieces, agg, wire = call(
        first_kernel,
        outs,
        [pltpu.VMEM(x.shape, x.dtype) for x in sources]
        + [pltpu.SemaphoreType.DMA((len(sources),))]
        + [pltpu.VMEM(*out) for out in outs]
        + [
            pltpu.SemaphoreType.DMA((2 + blocks,)),
            pltpu.VMEM((blocks, rows + 2 * LANES, width), BF16),
            pltpu.VMEM((blocks, LANES * piece, rows + 2 * LANES), BF16),
        ],
        far=len(sources),
        limit=60,
        flops=2 * devices * piece * rows * width,
        bytes_accessed=devices * piece * width * 2,
    )(*sources)
    recv = jnp.pad(receive_slots[0, 0], ((0, 0), (0, 0), (0, EXTRA)), constant_values=rows)
    total, targets = call(
        local_kernel,
        [((rows, width), F32), ((devices * piece // LANES, LANES), jnp.int32)],
        [pltpu.VMEM((rows, rows), BF16)],
        flops=2 * rows * rows * width,
        bytes_accessed=rows * width * 10,
    )(lists, recv.reshape(-1, LANES), wire, agg)

    def exchange(x, height):
        x = x.reshape(devices, height // 2, 2, width)
        return lax.all_to_all(x, AXES, split_axis=0, concat_axis=0, tiled=True).reshape(-1, width)

    arrived = exchange(pieces, piece)
    (share,) = call(
        functools.partial(chunk_kernel, piece, 1.0 / devices),
        [((devices * EXTRA, width), BF16)],
        flops=2 * 16 * devices * piece * width,
        bytes_accessed=devices * piece * width * 2,
    )(arrived)
    shares = exchange(share, EXTRA)
    (grad_x,) = call(
        remote_kernel,
        [((rows, width), BF16)],
        flops=2 * devices * piece * rows * width,
        bytes_accessed=devices * piece * width * 2,
    )(targets, arrived, total)
    w1, b1, w2, b2, node = call(
        last_kernel,
        [
            ((width, hidden), F32),
            ((1, hidden), F32),
            ((hidden, width), F32),
            ((1, width), F32),
            ((1, width), F32),
        ],
        [pltpu.VMEM((devices * EXTRA, width), F32)],
        flops=0,
        bytes_accessed=devices * EXTRA * width * 2,
    )(shares)
    return grad_x, w1, b1[0], w2, b2[0], node[0]


def solution(mesh):
    placed = (
        P(AXES, None),
        P(AXES, None),
        P(AXES, None),
        P(),
        P(),
        P(AXES, None),
        P("nodes", "grp", None, None, None),
        P("nodes", "grp", None, None, None),
    )
    return jax.shard_map(
        per_device,
        mesh=mesh,
        in_specs=placed,
        out_specs=(P(AXES, None), P(), P(), P(), P(), P()),
        check_vma=False,
    )
```

```python
import functools

import jax
import jax.numpy as jnp
from jax import lax
from jax.experimental import pallas as pl
from jax.experimental.pallas import tpu as pltpu
from jax.sharding import PartitionSpec as P

BF16 = jnp.bfloat16
F32 = jnp.float32
PLAIN = (((1,), (0,)), ((), ()))
LAST = (((1,), (1,)), ((), ()))
FIRST = (((0,), (0,)), ((), ()))
LANES = 128
EXTRA = 2
AXES = ("nodes", "grp")


def dot(a, b, dims=PLAIN):
    return lax.dot_general(a, b, dims, preferred_element_type=F32)


def iota(shape, dim):
    return lax.broadcasted_iota(jnp.int32, shape, dim)


def match(a, b):
    shape = jnp.broadcast_shapes(a.shape, b.shape)
    return jnp.where(a == b, jnp.ones(shape, BF16), jnp.zeros(shape, BF16))


def low_part(value):
    return value - value.astype(BF16).astype(F32)


def columns(row):
    return jnp.broadcast_to(row, (LANES, LANES)).T


def remainders(wide, thin):
    lane = iota(wide.shape, 1)
    low = jnp.where(lane == LANES - 2, thin, low_part(wide))
    return jnp.where(lane == LANES - 1, low_part(thin), low).astype(BF16)


def first_kernel(
    send_hbm, out_hbm, w2_hbm, hid_hbm, w1_hbm, lists_hbm, saved_hbm,
    piece_hbm, agg_hbm, wire_hbm,
    send_ref, out_ref, w2_ref, hid_ref, w1_ref, lists_ref, saved_ref, in_sems,
    piece_ref, agg_ref, wire_ref, out_sems,
    rows_ref, chosen_ref, index_ref,
):
    groups, slots, nodes = send_ref.shape
    rows = out_ref.shape[0]
    piece = slots + EXTRA
    block = LANES * piece
    width = LANES // groups
    blocks = nodes // width
    pairs = [
        (send_hbm, send_ref), (out_hbm, out_ref), (w2_hbm, w2_ref), (hid_hbm, hid_ref),
        (w1_hbm, w1_ref), (lists_hbm, lists_ref), (saved_hbm, saved_ref),
    ]
    arrivals = [pltpu.make_async_copy(a, b, in_sems.at[i]) for i, (a, b) in enumerate(pairs)]
    for copy in arrivals:
        copy.start()

    half = rows // 2
    place = jnp.where(
        iota((block, LANES), 0) // piece * piece == piece * iota((block, LANES), 1), 1.0, 0.0
    )
    place = jnp.where(iota((block, LANES), 0) % piece >= slots, place, 0.0).astype(BF16)
    for step in range(blocks):
        chosen_ref[step, :, half:] = place

    arrivals[0].wait()
    parts = []
    for g in range(groups):
        parts += [send_ref[g], jnp.full((1, nodes), -1, jnp.int32), jnp.full((1, nodes), 2 * rows, jnp.int32)]
    sent = jnp.concatenate(parts, axis=0)
    sent = jnp.concatenate([sent, pltpu.roll(sent, nodes - 1, 1)], axis=0).astype(jnp.int16)
    lane_index = iota((16, half), 1).astype(jnp.int16)

    def choose(step):
        for n in range(0, width, 2):
            for r in range(0, 2 * groups * piece, 16):
                at = step * width + n
                start = n * groups * piece + r
                index = jnp.broadcast_to(sent[r : r + 16, at : at + 1], (16, LANES))
                index_ref[step, start : start + 16, :] = index
                folded = jnp.where(index >= half, index - half, index)
                for t in range(0, half, LANES):
                    chosen_ref[step, start : start + 16, t : t + LANES] = match(folded, lane_index[:, t : t + LANES])

    choose(0)
    for copy in arrivals[1:5]:
        copy.wait()
    out = out_ref[...]
    hidden = hid_ref[...]
    grad_hidden = dot(out, w2_ref[...], LAST)
    grad_z = jnp.where(hidden > 0, grad_hidden, 0.0).astype(BF16)
    grad_agg = dot(grad_z, w1_ref[...], LAST)
    wire = grad_agg.astype(BF16)
    agg_ref[...] = grad_agg
    wire_ref[...] = wire
    departures = [
        pltpu.make_async_copy(agg_ref, agg_hbm, out_sems.at[0]),
        pltpu.make_async_copy(wire_ref, wire_hbm, out_sems.at[1]),
    ]
    for copy in departures:
        copy.start()
    for step in range(blocks):
        rows_ref[step, :half, :LANES] = wire[:half]
        rows_ref[step, :half, LANES:] = wire[half:]
    for copy in arrivals[5:]:
        copy.wait()

    few = 32
    row_index = iota((few, 1), 0).astype(jnp.int16)
    count = jnp.zeros((few, few), F32)
    for ref in [lists_ref] + [send_ref.at[g] for g in range(groups)]:
        index = ref[...]
        low = (index & (few - 1)).astype(jnp.int16)
        high = (index >> 5).astype(jnp.int16)
        for k in range(index.shape[0]):
            count += dot(match(low[k : k + 1], row_index), match(high[k : k + 1], row_index), LAST)
    carried = jnp.zeros((few, out.shape[1]), F32)
    for h in range(rows // few):
        carried += wire[h * few : (h + 1) * few].astype(F32) * count[:, h : h + 1]
    node = jnp.sum(grad_agg, axis=0, keepdims=True) + jnp.sum(carried, axis=0, keepdims=True)

    part_w1 = dot(saved_ref[...], grad_z, FIRST)
    part_w2 = dot(out, hidden, FIRST)
    sum_z = jnp.sum(grad_z.astype(F32), axis=0, keepdims=True)
    sum_out = jnp.sum(out.astype(F32), axis=0, keepdims=True)
    quarters = [
        (part_w1[:, :LANES], sum_z[:, :LANES]),
        (part_w1[:, LANES:], sum_z[:, LANES:]),
        (part_w2[:, :LANES], sum_out),
        (part_w2[:, LANES:], node),
    ]

    for step, (wide, thin) in enumerate(quarters):
        if step:
            choose(step)
        rows_ref[step, half:, :LANES] = wide.astype(BF16)
        rows_ref[step, half:, LANES:] = remainders(wide, columns(thin))
        own = pl.ds(step * block, block)
        both = dot(chosen_ref[step], rows_ref[step]).astype(BF16)
        piece_ref[own, :] = jnp.where(index_ref[step] >= half, both[:, LANES:], both[:, :LANES])
        copy = pltpu.make_async_copy(piece_ref.at[own], piece_hbm.at[own], out_sems.at[2 + step])
        copy.start()
        departures.append(copy)
    for copy in departures:
        copy.wait()


def local_kernel(lists_ref, recv_ref, wire_ref, agg_ref, total_ref, target_ref, counts_ref):
    rows = wire_ref.shape[0]
    row_index = iota((rows, 1), 0).astype(jnp.int16)
    for tile in range(rows // LANES):
        lists = lists_ref[:, tile * LANES : (tile + 1) * LANES].astype(jnp.int16)
        counts = match(lists[0:1], row_index)
        for k in range(1, lists_ref.shape[0]):
            counts += match(lists[k : k + 1], row_index)
        counts_ref[:, tile * LANES : (tile + 1) * LANES] = counts
    local = dot(wire_ref[...].T, counts_ref[...])
    total_ref[...] = agg_ref[...] + local.T
    target_ref[...] = recv_ref[...]


def chunk_kernel(piece, scale, arrived_ref, share_ref):
    span = piece * LANES
    lane = iota((16, span), 1)
    place = lane - piece * ((lane * ((1 << 16) // piece + 1)) >> 16)
    pick = jnp.where(place == piece - EXTRA + iota((16, span), 0), 1.0, 0.0).astype(BF16)
    sums = jnp.zeros((16, LANES), F32)
    for start in range(0, arrived_ref.shape[0], span):
        sums += dot(pick, arrived_ref[start : start + span, :])
    high, low = sums[0:1], sums[1:2]
    lane = iota(high.shape, 1)
    last = jnp.sum(jnp.where(lane >= LANES - 2, low, 0.0), axis=1, keepdims=True)
    wide = scale * (high + jnp.where(lane >= LANES - 2, 0.0, low))
    thin = jnp.broadcast_to(scale * last, wide.shape)
    pair = jnp.concatenate([wide.astype(BF16), remainders(wide, thin)], axis=0)
    share_ref[...] = jnp.concatenate([pair] * (share_ref.shape[0] // EXTRA), axis=0)


def remote_kernel(recv_ref, arrived_ref, total_ref, x_ref):
    rows = total_ref.shape[0]
    row_index = iota((rows, 1), 0).astype(jnp.int16)
    targets = recv_ref[...].astype(jnp.int16)
    total = total_ref[...]
    for r in range(0, recv_ref.shape[0], 2):
        chosen = jnp.concatenate([match(targets[q : q + 1], row_index) for q in (r, r + 1)], axis=1)
        total += dot(chosen, arrived_ref[r * LANES : (r + 2) * LANES, :])
    x_ref[...] = total.astype(BF16)


def last_kernel(share_ref, w1_ref, b1_ref, w2_ref, b2_ref, node_ref, rows_ref):
    rows_ref[...] = share_ref[...].astype(F32)
    half = rows_ref.shape[0] // 2
    high = rows_ref[pl.ds(0, half, 2), :]
    low = rows_ref[pl.ds(1, half, 2), :]
    lane = iota(high.shape, 1)
    wide = high + jnp.where(lane >= LANES - 2, 0.0, low)
    w1_ref[:, :LANES] = wide[:LANES]
    w1_ref[:, LANES:] = wide[LANES : 2 * LANES]
    w2_ref[:LANES, :] = wide[2 * LANES : 3 * LANES].T
    w2_ref[LANES:, :] = wide[3 * LANES :].T
    thin = []
    for q in range(4):
        turned = low[q * LANES : (q + 1) * LANES].T
        thin.append(turned[LANES - 2 : LANES - 1] + turned[LANES - 1 :])
    b1_ref[...] = jnp.concatenate(thin[:2], axis=1)
    b2_ref[...] = thin[2]
    node_ref[...] = thin[3]


def call(kernel, outs, scratch=(), far=0, limit=24, **cost):
    hbm = pl.BlockSpec(memory_space=pltpu.HBM)
    specs = {"in_specs": [hbm] * far, "out_specs": [hbm] * len(outs)} if far else {}
    return pl.pallas_call(
        kernel,
        out_shape=[jax.ShapeDtypeStruct(shape, dtype) for shape, dtype in outs],
        scratch_shapes=list(scratch),
        compiler_params=pltpu.CompilerParams(vmem_limit_bytes=limit << 20),
        cost_estimate=pl.CostEstimate(transcendentals=0, **cost),
        **specs,
    )


def per_device(
    grad_out, agg_saved, hidden_saved, w_one, w_two, local_lists, send_slots, receive_slots
):
    rows, width = grad_out.shape
    hidden = hidden_saved.shape[1]
    nodes, groups, slots = send_slots.shape[2:]
    devices = nodes * groups
    piece = slots + EXTRA
    lists = local_lists.T
    send = jnp.transpose(send_slots[0, 0], (1, 2, 0))
    sources = [send, grad_out, w_two, hidden_saved, w_one, lists, agg_saved]
    outs = [((devices * piece, width), BF16), ((rows, width), F32), ((rows, width), BF16)]
    blocks = devices // LANES
    pieces, agg, wire = call(
        first_kernel,
        outs,
        [pltpu.VMEM(x.shape, x.dtype) for x in sources]
        + [pltpu.SemaphoreType.DMA((len(sources),))]
        + [pltpu.VMEM(*out) for out in outs]
        + [
            pltpu.SemaphoreType.DMA((2 + blocks,)),
            pltpu.VMEM((blocks, rows // 2 + LANES, 2 * width), BF16),
            pltpu.VMEM((blocks, LANES * piece, rows // 2 + LANES), BF16),
            pltpu.VMEM((blocks, LANES * piece, LANES), jnp.int16),
        ],
        far=len(sources),
        limit=60,
        flops=2 * devices * piece * rows * width,
        bytes_accessed=devices * piece * width * 2,
    )(*sources)
    recv = jnp.pad(receive_slots[0, 0], ((0, 0), (0, 0), (0, EXTRA)), constant_values=rows)
    total, targets = call(
        local_kernel,
        [((rows, width), F32), ((devices * piece // LANES, LANES), jnp.int32)],
        [pltpu.VMEM((rows, rows), BF16)],
        flops=2 * rows * rows * width,
        bytes_accessed=rows * width * 10,
    )(lists, recv.reshape(-1, LANES), wire, agg)

    def exchange(x, height):
        x = x.reshape(devices, height // 2, 2, width)
        return lax.all_to_all(x, AXES, split_axis=0, concat_axis=0, tiled=True).reshape(-1, width)

    arrived = exchange(pieces, piece)
    (share,) = call(
        functools.partial(chunk_kernel, piece, 1.0 / devices),
        [((devices * EXTRA, width), BF16)],
        flops=2 * 16 * devices * piece * width,
        bytes_accessed=devices * piece * width * 2,
    )(arrived)
    shares = exchange(share, EXTRA)
    (grad_x,) = call(
        remote_kernel,
        [((rows, width), BF16)],
        flops=2 * devices * piece * rows * width,
        bytes_accessed=devices * piece * width * 2,
    )(targets, arrived, total)
    w1, b1, w2, b2, node = call(
        last_kernel,
        [
            ((width, hidden), F32),
            ((1, hidden), F32),
            ((hidden, width), F32),
            ((1, width), F32),
            ((1, width), F32),
        ],
        [pltpu.VMEM((devices * EXTRA, width), F32)],
        flops=0,
        bytes_accessed=devices * EXTRA * width * 2,
    )(shares)
    return grad_x, w1, b1[0], w2, b2[0], node[0]


def solution(mesh):
    placed = (
        P(AXES, None),
        P(AXES, None),
        P(AXES, None),
        P(),
        P(),
        P(AXES, None),
        P("nodes", "grp", None, None, None),
        P("nodes", "grp", None, None, None),
    )
    return jax.shard_map(
        per_device,
        mesh=mesh,
        in_specs=placed,
        out_specs=(P(AXES, None), P(), P(), P(), P(), P()),
        check_vma=False,
    )
```

```python
import functools

import jax
import jax.numpy as jnp
from jax import lax
from jax.experimental import pallas as pl
from jax.experimental.pallas import tpu as pltpu
from jax.sharding import PartitionSpec as P

BF16 = jnp.bfloat16
F32 = jnp.float32
PLAIN = (((1,), (0,)), ((), ()))
LAST = (((1,), (1,)), ((), ()))
FIRST = (((0,), (0,)), ((), ()))
LANES = 128
EXTRA = 2
AXES = ("nodes", "grp")


def dot(a, b, dims=PLAIN):
    return lax.dot_general(a, b, dims, preferred_element_type=F32)


def iota(shape, dim):
    return lax.broadcasted_iota(jnp.int32, shape, dim)


def match(a, b):
    shape = jnp.broadcast_shapes(a.shape, b.shape)
    return jnp.where(a == b, jnp.ones(shape, BF16), jnp.zeros(shape, BF16))


def low_part(value):
    return value - value.astype(BF16).astype(F32)


def columns(row):
    return jnp.broadcast_to(row, (LANES, LANES)).T


def remainders(wide, thin):
    lane = iota(wide.shape, 1)
    low = jnp.where(lane == LANES - 2, thin, low_part(wide))
    return jnp.where(lane == LANES - 1, low_part(thin), low).astype(BF16)


def choose(half, steps, send_ref, chosen_ref, index_ref):
    groups, slots, nodes = send_ref.shape
    block = chosen_ref.shape[1]
    piece = slots + EXTRA
    width = LANES // groups
    place = jnp.where(
        iota((block, LANES), 0) // piece * piece == piece * iota((block, LANES), 1), 1.0, 0.0
    )
    place = jnp.where(iota((block, LANES), 0) % piece >= slots, place, 0.0).astype(BF16)
    parts = []
    for g in range(groups):
        parts += [send_ref[g], jnp.full((1, nodes), -1, jnp.int32), jnp.full((1, nodes), 4 * half, jnp.int32)]
    sent = jnp.concatenate(parts, axis=0)
    sent = jnp.concatenate([sent, pltpu.roll(sent, nodes - 1, 1)], axis=0).astype(jnp.int16)
    lane_index = iota((16, half), 1).astype(jnp.int16)
    for i, step in enumerate(steps):
        chosen_ref[i, :, half:] = place
        for n in range(0, width, 2):
            for r in range(0, 2 * groups * piece, 16):
                at = step * width + n
                start = n * groups * piece + r
                index = jnp.broadcast_to(sent[r : r + 16, at : at + 1], (16, LANES))
                index_ref[i, start : start + 16, :] = index
                folded = jnp.where(index >= half, index - half, index)
                for t in range(0, half, LANES):
                    chosen_ref[i, start : start + 16, t : t + LANES] = match(folded, lane_index[:, t : t + LANES])


def first_kernel(
    chosen_ref, index_ref, send_ref, out_ref, w2_ref, hid_ref, w1_ref, lists_ref, saved_ref,
    piece_ref, agg_ref, wire_ref, rows_ref, more_chosen_ref, more_index_ref,
):
    early, block, _ = chosen_ref.shape
    blocks = rows_ref.shape[0]
    groups = send_ref.shape[0]
    rows = out_ref.shape[0]
    half = rows // 2
    out = out_ref[...]
    hidden = hid_ref[...]
    grad_hidden = dot(out, w2_ref[...], LAST)
    grad_z = jnp.where(hidden > 0, grad_hidden, 0.0).astype(BF16)
    grad_agg = dot(grad_z, w1_ref[...], LAST)
    wire = grad_agg.astype(BF16)
    agg_ref[...] = grad_agg
    wire_ref[...] = wire
    for step in range(blocks):
        rows_ref[step, :half, :LANES] = wire[:half]
        rows_ref[step, :half, LANES:] = wire[half:]
    choose(half, range(early, blocks), send_ref, more_chosen_ref, more_index_ref)

    few = 32
    row_index = iota((few, 1), 0).astype(jnp.int16)
    count = jnp.zeros((few, few), F32)
    for ref in [lists_ref] + [send_ref.at[g] for g in range(groups)]:
        index = ref[...]
        low = (index & (few - 1)).astype(jnp.int16)
        high = (index >> 5).astype(jnp.int16)
        for k in range(index.shape[0]):
            count += dot(match(low[k : k + 1], row_index), match(high[k : k + 1], row_index), LAST)
    carried = jnp.zeros((few, out.shape[1]), F32)
    for h in range(rows // few):
        carried += wire[h * few : (h + 1) * few].astype(F32) * count[:, h : h + 1]
    node = jnp.sum(grad_agg, axis=0, keepdims=True) + jnp.sum(carried, axis=0, keepdims=True)

    part_w1 = dot(saved_ref[...], grad_z, FIRST)
    part_w2 = dot(out, hidden, FIRST)
    sum_z = jnp.sum(grad_z.astype(F32), axis=0, keepdims=True)
    sum_out = jnp.sum(out.astype(F32), axis=0, keepdims=True)
    quarters = [
        (part_w1[:, :LANES], sum_z[:, :LANES]),
        (part_w1[:, LANES:], sum_z[:, LANES:]),
        (part_w2[:, :LANES], sum_out),
        (part_w2[:, LANES:], node),
    ]

    for step, (wide, thin) in enumerate(quarters):
        rows_ref[step, half:, :LANES] = wide.astype(BF16)
        rows_ref[step, half:, LANES:] = remainders(wide, columns(thin))
        selects, indices = (chosen_ref, index_ref) if step < early else (more_chosen_ref, more_index_ref)
        at = step if step < early else step - early
        both = dot(selects[at], rows_ref[step]).astype(BF16)
        piece_ref[step * block : (step + 1) * block, :] = jnp.where(
            indices[at] >= half, both[:, LANES:], both[:, :LANES]
        )


def local_kernel(lists_ref, recv_ref, wire_ref, agg_ref, total_ref, target_ref, counts_ref):
    rows = wire_ref.shape[0]
    row_index = iota((rows, 1), 0).astype(jnp.int16)
    for tile in range(rows // LANES):
        lists = lists_ref[:, tile * LANES : (tile + 1) * LANES].astype(jnp.int16)
        counts = match(lists[0:1], row_index)
        for k in range(1, lists_ref.shape[0]):
            counts += match(lists[k : k + 1], row_index)
        counts_ref[:, tile * LANES : (tile + 1) * LANES] = counts
    local = dot(wire_ref[...].T, counts_ref[...])
    total_ref[...] = agg_ref[...] + local.T
    target_ref[...] = recv_ref[...]


def chunk_kernel(piece, scale, arrived_ref, share_ref):
    span = piece * LANES
    lane = iota((16, span), 1)
    place = lane - piece * ((lane * ((1 << 16) // piece + 1)) >> 16)
    pick = jnp.where(place == piece - EXTRA + iota((16, span), 0), 1.0, 0.0).astype(BF16)
    sums = jnp.zeros((16, LANES), F32)
    for start in range(0, arrived_ref.shape[0], span):
        sums += dot(pick, arrived_ref[start : start + span, :])
    high, low = sums[0:1], sums[1:2]
    lane = iota(high.shape, 1)
    last = jnp.sum(jnp.where(lane >= LANES - 2, low, 0.0), axis=1, keepdims=True)
    wide = scale * (high + jnp.where(lane >= LANES - 2, 0.0, low))
    thin = jnp.broadcast_to(scale * last, wide.shape)
    pair = jnp.concatenate([wide.astype(BF16), remainders(wide, thin)], axis=0)
    share_ref[...] = jnp.concatenate([pair] * (share_ref.shape[0] // EXTRA), axis=0)


def remote_kernel(recv_ref, arrived_ref, total_ref, x_ref):
    rows = total_ref.shape[0]
    row_index = iota((rows, 1), 0).astype(jnp.int16)
    targets = recv_ref[...].astype(jnp.int16)
    total = total_ref[...]
    for r in range(0, recv_ref.shape[0], 2):
        chosen = jnp.concatenate([match(targets[q : q + 1], row_index) for q in (r, r + 1)], axis=1)
        total += dot(chosen, arrived_ref[r * LANES : (r + 2) * LANES, :])
    x_ref[...] = total.astype(BF16)


def last_kernel(share_ref, w1_ref, b1_ref, w2_ref, b2_ref, node_ref, rows_ref):
    rows_ref[...] = share_ref[...].astype(F32)
    half = rows_ref.shape[0] // 2
    high = rows_ref[pl.ds(0, half, 2), :]
    low = rows_ref[pl.ds(1, half, 2), :]
    lane = iota(high.shape, 1)
    wide = high + jnp.where(lane >= LANES - 2, 0.0, low)
    w1_ref[:, :LANES] = wide[:LANES]
    w1_ref[:, LANES:] = wide[LANES : 2 * LANES]
    w2_ref[:LANES, :] = wide[2 * LANES : 3 * LANES].T
    w2_ref[LANES:, :] = wide[3 * LANES :].T
    thin = []
    for q in range(4):
        turned = low[q * LANES : (q + 1) * LANES].T
        thin.append(turned[LANES - 2 : LANES - 1] + turned[LANES - 1 :])
    b1_ref[...] = jnp.concatenate(thin[:2], axis=1)
    b2_ref[...] = thin[2]
    node_ref[...] = thin[3]


def call(kernel, outs, scratch=(), limit=24, **cost):
    return pl.pallas_call(
        kernel,
        out_shape=[jax.ShapeDtypeStruct(shape, dtype) for shape, dtype in outs],
        scratch_shapes=list(scratch),
        compiler_params=pltpu.CompilerParams(vmem_limit_bytes=limit << 20),
        cost_estimate=pl.CostEstimate(transcendentals=0, **cost),
    )


def per_device(
    grad_out, agg_saved, hidden_saved, w_one, w_two, local_lists, send_slots, receive_slots
):
    rows, width = grad_out.shape
    hidden = hidden_saved.shape[1]
    nodes, groups, slots = send_slots.shape[2:]
    devices = nodes * groups
    piece = slots + EXTRA
    lists = local_lists.T
    send = jnp.transpose(send_slots[0, 0], (1, 2, 0))
    blocks = devices // LANES
    depth = rows // 2 + LANES
    early = blocks // 2

    def shapes(n):
        return [((n, LANES * piece, depth), BF16), ((n, LANES * piece, LANES), jnp.int16)]

    chosen, index = call(
        functools.partial(choose, rows // 2, range(early)),
        shapes(early),
        flops=2 * 10**9,
        bytes_accessed=early * LANES * piece * depth * 2,
        limit=8,
    )(send)
    pieces, agg, wire = call(
        first_kernel,
        [((devices * piece, width), BF16), ((rows, width), F32), ((rows, width), BF16)],
        [pltpu.VMEM((blocks, depth, 2 * width), BF16)]
        + [pltpu.VMEM(*shape) for shape in shapes(blocks - early)],
        limit=16,
        flops=4 * devices * piece * depth * width,
        bytes_accessed=devices * piece * depth * 2,
    )(chosen, index, send, grad_out, w_two, hidden_saved, w_one, lists, agg_saved)
    recv = jnp.pad(receive_slots[0, 0], ((0, 0), (0, 0), (0, EXTRA)), constant_values=rows)
    total, targets = call(
        local_kernel,
        [((rows, width), F32), ((devices * piece // LANES, LANES), jnp.int32)],
        [pltpu.VMEM((rows, rows), BF16)],
        flops=2 * rows * rows * width,
        bytes_accessed=rows * width * 10,
    )(lists, recv.reshape(-1, LANES), wire, agg)

    def exchange(x, height):
        x = x.reshape(devices, height // 2, 2, width)
        return lax.all_to_all(x, AXES, split_axis=0, concat_axis=0, tiled=True).reshape(-1, width)

    arrived = exchange(pieces, piece)
    (share,) = call(
        functools.partial(chunk_kernel, piece, 1.0 / devices),
        [((devices * EXTRA, width), BF16)],
        flops=2 * 16 * devices * piece * width,
        bytes_accessed=devices * piece * width * 2,
    )(arrived)
    shares = exchange(share, EXTRA)
    (grad_x,) = call(
        remote_kernel,
        [((rows, width), BF16)],
        flops=2 * devices * piece * rows * width,
        bytes_accessed=devices * piece * width * 2,
    )(targets, arrived, total)
    w1, b1, w2, b2, node = call(
        last_kernel,
        [
            ((width, hidden), F32),
            ((1, hidden), F32),
            ((hidden, width), F32),
            ((1, width), F32),
            ((1, width), F32),
        ],
        [pltpu.VMEM((devices * EXTRA, width), F32)],
        flops=0,
        bytes_accessed=devices * EXTRA * width * 2,
    )(shares)
    return grad_x, w1, b1[0], w2, b2[0], node[0]


def solution(mesh):
    placed = (
        P(AXES, None),
        P(AXES, None),
        P(AXES, None),
        P(),
        P(),
        P(AXES, None),
        P("nodes", "grp", None, None, None),
        P("nodes", "grp", None, None, None),
    )
    return jax.shard_map(
        per_device,
        mesh=mesh,
        in_specs=placed,
        out_specs=(P(AXES, None), P(), P(), P(), P(), P()),
        check_vma=False,
    )
```

```python
import functools

import jax
import jax.numpy as jnp
from jax import lax
from jax.experimental import pallas as pl
from jax.experimental.pallas import tpu as pltpu
from jax.sharding import Mesh
from jax.sharding import PartitionSpec as P

BF16 = jnp.bfloat16
F32 = jnp.float32
PLAIN = (((1,), (0,)), ((), ()))
LAST = (((1,), (1,)), ((), ()))
FIRST = (((0,), (0,)), ((), ()))
LANES = 128
EXTRA = 2
CORES = 2
AXES = ("chips", "core", "grp")


def dot(a, b, dims=PLAIN):
    return lax.dot_general(a, b, dims, preferred_element_type=F32)


def iota(shape, dim):
    return lax.broadcasted_iota(jnp.int32, shape, dim)


def match(a, b):
    shape = jnp.broadcast_shapes(a.shape, b.shape)
    return jnp.where(a == b, jnp.ones(shape, BF16), jnp.zeros(shape, BF16))


def low_part(value):
    return value - value.astype(BF16).astype(F32)


def columns(row):
    return jnp.broadcast_to(row, (LANES, LANES)).T


def remainders(wide, thin):
    lane = iota(wide.shape, 1)
    low = jnp.where(lane == LANES - 2, thin, low_part(wide))
    return jnp.where(lane == LANES - 1, low_part(thin), low).astype(BF16)


def choose(half, steps, send_ref, chosen_ref, index_ref):
    groups, slots, nodes = send_ref.shape
    block = chosen_ref.shape[1]
    piece = slots + EXTRA
    width = LANES // groups
    row, lane = iota((block, LANES), 0), iota((block, LANES), 1)
    share = LANES // CORES
    owner = (lane % share // groups * CORES + lane // share) * groups + lane % groups
    place = jnp.where(row // piece == owner, 1.0, 0.0)
    place = jnp.where(row % piece >= slots, place, 0.0).astype(BF16)
    parts = []
    for g in range(groups):
        parts += [send_ref[g], jnp.full((1, nodes), -1, jnp.int32), jnp.full((1, nodes), 4 * half, jnp.int32)]
    sent = jnp.concatenate(parts, axis=0)
    sent = jnp.concatenate([sent, pltpu.roll(sent, nodes - 1, 1)], axis=0).astype(jnp.int16)
    lane_index = iota((16, half), 1).astype(jnp.int16)
    for i, step in enumerate(steps):
        chosen_ref[i, :, half:] = place
        for n in range(0, width, 2):
            for r in range(0, 2 * groups * piece, 16):
                at = step * width + n
                start = n * groups * piece + r
                index = jnp.broadcast_to(sent[r : r + 16, at : at + 1], (16, LANES))
                index_ref[i, start : start + 16, :] = index
                folded = jnp.where(index >= half, index - half, index)
                for t in range(0, half, LANES):
                    chosen_ref[i, start : start + 16, t : t + LANES] = match(folded, lane_index[:, t : t + LANES])


def first_kernel(
    chosen_ref, index_ref, send_ref, out_ref, w2_ref, hid_ref, w1_ref, lists_ref, saved_ref,
    piece_ref, agg_ref, wire_ref, rows_ref, more_chosen_ref, more_index_ref,
):
    early, block, _ = chosen_ref.shape
    blocks = rows_ref.shape[0]
    groups = send_ref.shape[0]
    rows = out_ref.shape[0]
    half = rows // 2
    out = out_ref[...]
    hidden = hid_ref[...]
    grad_hidden = dot(out, w2_ref[...], LAST)
    grad_z = jnp.where(hidden > 0, grad_hidden, 0.0).astype(BF16)
    grad_agg = dot(grad_z, w1_ref[...], LAST)
    wire = grad_agg.astype(BF16)
    agg_ref[...] = grad_agg
    wire_ref[...] = wire
    for step in range(blocks):
        rows_ref[step, :half, :LANES] = wire[:half]
        rows_ref[step, :half, LANES:] = wire[half:]
    choose(half, range(early, blocks), send_ref, more_chosen_ref, more_index_ref)

    few = 32
    row_index = iota((few, 1), 0).astype(jnp.int16)
    count = jnp.zeros((few, few), F32)
    for ref in [lists_ref] + [send_ref.at[g] for g in range(groups)]:
        index = ref[...]
        low = (index & (few - 1)).astype(jnp.int16)
        high = (index >> 5).astype(jnp.int16)
        for k in range(index.shape[0]):
            count += dot(match(low[k : k + 1], row_index), match(high[k : k + 1], row_index), LAST)
    carried = jnp.zeros((few, out.shape[1]), F32)
    for h in range(rows // few):
        carried += wire[h * few : (h + 1) * few].astype(F32) * count[:, h : h + 1]
    node = jnp.sum(grad_agg, axis=0, keepdims=True) + jnp.sum(carried, axis=0, keepdims=True)

    part_w1 = dot(saved_ref[...], grad_z, FIRST)
    part_w2 = dot(out, hidden, FIRST)
    sum_z = jnp.sum(grad_z.astype(F32), axis=0, keepdims=True)
    sum_out = jnp.sum(out.astype(F32), axis=0, keepdims=True)
    quarters = [
        (part_w1[:, :LANES], sum_z[:, :LANES]),
        (part_w1[:, LANES:], sum_z[:, LANES:]),
        (part_w2[:, :LANES], sum_out),
        (part_w2[:, LANES:], node),
    ]

    share = LANES // CORES
    for q, (wide, thin) in enumerate(quarters):
        high, low = wide.astype(BF16), remainders(wide, columns(thin))
        core, first = q // 2, q % 2 * CORES
        for c in range(CORES):
            to = slice(half + core * share, half + (core + 1) * share)
            rows_ref[first + c, to, :LANES] = high[c * share : (c + 1) * share]
            rows_ref[first + c, to, LANES:] = low[c * share : (c + 1) * share]
    for step in range(blocks):
        selects, indices = (chosen_ref, index_ref) if step < early else (more_chosen_ref, more_index_ref)
        at = step if step < early else step - early
        both = dot(selects[at], rows_ref[step]).astype(BF16)
        piece_ref[step * block : (step + 1) * block, :] = jnp.where(
            indices[at] >= half, both[:, LANES:], both[:, :LANES]
        )


def local_kernel(lists_ref, recv_ref, wire_ref, agg_ref, total_ref, target_ref, counts_ref):
    rows = wire_ref.shape[0]
    row_index = iota((rows, 1), 0).astype(jnp.int16)
    for tile in range(rows // LANES):
        lists = lists_ref[:, tile * LANES : (tile + 1) * LANES].astype(jnp.int16)
        counts = match(lists[0:1], row_index)
        for k in range(1, lists_ref.shape[0]):
            counts += match(lists[k : k + 1], row_index)
        counts_ref[:, tile * LANES : (tile + 1) * LANES] = counts
    local = dot(wire_ref[...].T, counts_ref[...])
    total_ref[...] = agg_ref[...] + local.T
    target_ref[...] = recv_ref[...]


def chunk_kernel(piece, scale, arrived_ref, share_ref):
    span = piece * LANES
    lane = iota((16, span), 1)
    place = lane - piece * ((lane * ((1 << 16) // piece + 1)) >> 16)
    pick = jnp.where(place == piece - EXTRA + iota((16, span), 0), 1.0, 0.0).astype(BF16)
    sums = jnp.zeros((16, LANES), F32)
    for start in range(0, arrived_ref.shape[0], span):
        sums += dot(pick, arrived_ref[start : start + span, :])
    high, low = sums[0:1], sums[1:2]
    lane = iota(high.shape, 1)
    last = jnp.sum(jnp.where(lane >= LANES - 2, low, 0.0), axis=1, keepdims=True)
    wide = scale * (high + jnp.where(lane >= LANES - 2, 0.0, low))
    thin = jnp.broadcast_to(scale * last, wide.shape)
    pair = jnp.concatenate([wide.astype(BF16), remainders(wide, thin)], axis=0)
    share_ref[...] = jnp.concatenate([pair] * (share_ref.shape[0] // EXTRA), axis=0)


def remote_kernel(recv_ref, arrived_ref, total_ref, x_ref):
    rows = total_ref.shape[0]
    row_index = iota((rows, 1), 0).astype(jnp.int16)
    targets = recv_ref[...].astype(jnp.int16)
    total = total_ref[...]
    for r in range(0, recv_ref.shape[0], 2):
        chosen = jnp.concatenate([match(targets[q : q + 1], row_index) for q in (r, r + 1)], axis=1)
        total += dot(chosen, arrived_ref[r * LANES : (r + 2) * LANES, :])
    x_ref[...] = total.astype(BF16)


def last_kernel(core_ref, mine_ref, mate_ref, w1_ref, b1_ref, w2_ref, b2_ref, node_ref, rows_ref):
    first = core_ref[0] == 0
    count = mine_ref.shape[0]
    mine, mate = mine_ref[...].astype(F32), mate_ref[...].astype(F32)
    rows_ref[:count, :] = jnp.where(first, mine, mate)
    rows_ref[count : 2 * count, :] = jnp.where(first, mate, mine)
    high = rows_ref[pl.ds(0, count, 2), :]
    low = rows_ref[pl.ds(1, count, 2), :]
    lane = iota(high.shape, 1)
    wide = high + jnp.where(lane >= LANES - 2, 0.0, low)
    w1_ref[:, :LANES] = wide[:LANES]
    w1_ref[:, LANES:] = wide[LANES : 2 * LANES]
    w2_ref[:LANES, :] = wide[2 * LANES : 3 * LANES].T
    w2_ref[LANES:, :] = wide[3 * LANES :].T
    thin = []
    for q in range(4):
        turned = low[q * LANES : (q + 1) * LANES].T
        thin.append(turned[LANES - 2 : LANES - 1] + turned[LANES - 1 :])
    b1_ref[...] = jnp.concatenate(thin[:2], axis=1)
    b2_ref[...] = thin[2]
    node_ref[...] = thin[3]


def call(kernel, outs, scratch=(), limit=24, specs=None, **cost):
    extra = {"in_specs": specs} if specs else {}
    return pl.pallas_call(
        kernel,
        out_shape=[jax.ShapeDtypeStruct(shape, dtype) for shape, dtype in outs],
        scratch_shapes=list(scratch),
        compiler_params=pltpu.CompilerParams(vmem_limit_bytes=limit << 20),
        cost_estimate=pl.CostEstimate(transcendentals=0, **cost),
        **extra,
    )


def per_device(
    grad_out, agg_saved, hidden_saved, w_one, w_two, local_lists, send_slots, receive_slots
):
    rows, width = grad_out.shape
    hidden = hidden_saved.shape[1]
    nodes, groups, slots = send_slots.shape[2:]
    devices = nodes * groups
    piece = slots + EXTRA
    lists = local_lists.T
    send = jnp.transpose(send_slots[0, 0], (1, 2, 0))
    blocks = devices // LANES
    depth = rows // 2 + LANES
    early = blocks // 2

    def shapes(n):
        return [((n, LANES * piece, depth), BF16), ((n, LANES * piece, LANES), jnp.int16)]

    chosen, index = call(
        functools.partial(choose, rows // 2, range(early)),
        shapes(early),
        flops=2 * 10**9,
        bytes_accessed=early * LANES * piece * depth * 2,
        limit=8,
    )(send)
    pieces, agg, wire = call(
        first_kernel,
        [((devices * piece, width), BF16), ((rows, width), F32), ((rows, width), BF16)],
        [pltpu.VMEM((blocks, depth, 2 * width), BF16)]
        + [pltpu.VMEM(*shape) for shape in shapes(blocks - early)],
        limit=16,
        flops=4 * devices * piece * depth * width,
        bytes_accessed=devices * piece * depth * 2,
    )(chosen, index, send, grad_out, w_two, hidden_saved, w_one, lists, agg_saved)
    recv = jnp.pad(receive_slots[0, 0], ((0, 0), (0, 0), (0, EXTRA)), constant_values=rows)
    total, targets = call(
        local_kernel,
        [((rows, width), F32), ((devices * piece // LANES, LANES), jnp.int32)],
        [pltpu.VMEM((rows, rows), BF16)],
        flops=2 * rows * rows * width,
        bytes_accessed=rows * width * 10,
    )(lists, recv.reshape(-1, LANES), wire, agg)

    def exchange(x, height, axes):
        x = x.reshape(-1, height // 2, 2, width)
        return lax.all_to_all(x, axes, split_axis=0, concat_axis=0, tiled=True).reshape(-1, width)

    arrived = exchange(pieces, piece, AXES)
    (share,) = call(
        functools.partial(chunk_kernel, piece, 1.0 / devices),
        [((devices // CORES * EXTRA, width), BF16)],
        flops=2 * 16 * devices * piece * width,
        bytes_accessed=devices * piece * width * 2,
    )(arrived)
    mine = exchange(share, EXTRA, ("chips", "grp"))
    (grad_x,) = call(
        remote_kernel,
        [((rows, width), BF16)],
        flops=2 * devices * piece * rows * width,
        bytes_accessed=devices * piece * width * 2,
    )(targets, arrived, total)
    grad_x, mine = lax.optimization_barrier((grad_x, mine))
    mate = lax.ppermute(mine, "core", [(c, CORES - 1 - c) for c in range(CORES)])
    w1, b1, w2, b2, node = call(
        last_kernel,
        [
            ((width, hidden), F32),
            ((1, hidden), F32),
            ((hidden, width), F32),
            ((1, width), F32),
            ((1, width), F32),
        ],
        [pltpu.VMEM((devices * EXTRA + 8, width), F32)],
        specs=[pl.BlockSpec(memory_space=pltpu.SMEM)] + [pl.BlockSpec(memory_space=pltpu.VMEM)] * 2,
        flops=0,
        bytes_accessed=devices * EXTRA * width * 2,
    )(lax.axis_index("core").astype(jnp.int32).reshape(1), mine, mate)
    return grad_x, w1, b1[0], w2, b2[0], node[0]


def solution(mesh):
    nodes, groups = mesh.devices.shape
    chips = Mesh(mesh.devices.reshape(nodes // CORES, CORES, groups), AXES)
    placed = (
        P(AXES, None),
        P(AXES, None),
        P(AXES, None),
        P(),
        P(),
        P(AXES, None),
        P(AXES[:2], "grp", None, None, None),
        P(AXES[:2], "grp", None, None, None),
    )
    return jax.shard_map(
        per_device,
        mesh=chips,
        in_specs=placed,
        out_specs=(P(AXES, None), P(), P(), P(), P(), P()),
        check_vma=False,
    )
```

```python
import functools

import jax
import jax.numpy as jnp
from jax import lax
from jax.experimental import pallas as pl
from jax.experimental.pallas import tpu as pltpu
from jax.sharding import PartitionSpec as P

BF16 = jnp.bfloat16
F32 = jnp.float32
PLAIN = (((1,), (0,)), ((), ()))
LAST = (((1,), (1,)), ((), ()))
FIRST = (((0,), (0,)), ((), ()))
LANES = 128
EXTRA = 2
AXES = ("nodes", "grp")


def dot(a, b, dims=PLAIN):
    return lax.dot_general(a, b, dims, preferred_element_type=F32)


def iota(shape, dim):
    return lax.broadcasted_iota(jnp.int32, shape, dim)


def match(a, b):
    shape = jnp.broadcast_shapes(a.shape, b.shape)
    return jnp.where(a == b, jnp.ones(shape, BF16), jnp.zeros(shape, BF16))


def low_part(value):
    return value - value.astype(BF16).astype(F32)


def columns(row):
    return jnp.broadcast_to(row, (LANES, LANES)).T


def remainders(wide, thin):
    lane = iota(wide.shape, 1)
    low = jnp.where(lane == LANES - 2, thin, low_part(wide))
    return jnp.where(lane == LANES - 1, low_part(thin), low).astype(BF16)


def choose(half, steps, send_ref, chosen_ref, index_ref):
    groups, slots, nodes = send_ref.shape
    block = chosen_ref.shape[1]
    piece = slots + EXTRA
    width = LANES // groups
    place = jnp.where(
        iota((block, LANES), 0) // piece * piece == piece * iota((block, LANES), 1), 1.0, 0.0
    )
    place = jnp.where(iota((block, LANES), 0) % piece >= slots, place, 0.0).astype(BF16)
    parts = []
    for g in range(groups):
        parts += [send_ref[g], jnp.full((1, nodes), -1, jnp.int32), jnp.full((1, nodes), 4 * half, jnp.int32)]
    sent = jnp.concatenate(parts, axis=0)
    sent = jnp.concatenate([sent, pltpu.roll(sent, nodes - 1, 1)], axis=0).astype(jnp.int16)
    lane_index = iota((16, half), 1).astype(jnp.int16)
    for i, step in enumerate(steps):
        chosen_ref[i, :, half:] = place
        for n in range(0, width, 2):
            for r in range(0, 2 * groups * piece, 16):
                at = step * width + n
                start = n * groups * piece + r
                index = jnp.broadcast_to(sent[r : r + 16, at : at + 1], (16, LANES))
                index_ref[i, start : start + 16, :] = index
                folded = jnp.where(index >= half, index - half, index)
                for t in range(0, half, LANES):
                    chosen_ref[i, start : start + 16, t : t + LANES] = match(folded, lane_index[:, t : t + LANES])


def first_kernel(
    chosen_ref, index_ref, send_ref, out_ref, w2_ref, hid_ref, w1_ref, lists_ref, saved_ref,
    piece_ref, agg_ref, wire_ref, rows_ref, more_chosen_ref, more_index_ref,
):
    early, block, _ = chosen_ref.shape
    blocks = rows_ref.shape[0]
    groups = send_ref.shape[0]
    rows = out_ref.shape[0]
    half = rows // 2
    out = out_ref[...]
    hidden = hid_ref[...]
    grad_hidden = dot(out, w2_ref[...], LAST)
    part_w2 = dot(out, hidden, FIRST)
    grad_z = jnp.where(hidden > 0, grad_hidden, 0.0).astype(BF16)
    grad_agg = dot(grad_z, w1_ref[...], LAST)
    wire = grad_agg.astype(BF16)
    agg_ref[...] = grad_agg
    wire_ref[...] = wire
    for step in range(blocks):
        rows_ref[step, :half, :LANES] = wire[:half]
        rows_ref[step, :half, LANES:] = wire[half:]
    choose(half, range(early, blocks), send_ref, more_chosen_ref, more_index_ref)

    few = 32
    row_index = iota((few, 1), 0).astype(jnp.int16)
    count = jnp.zeros((few, few), F32)
    for ref in [lists_ref] + [send_ref.at[g] for g in range(groups)]:
        index = ref[...]
        low = (index & (few - 1)).astype(jnp.int16)
        high = (index >> 5).astype(jnp.int16)
        for k in range(index.shape[0]):
            count += dot(match(low[k : k + 1], row_index), match(high[k : k + 1], row_index), LAST)
    carried = jnp.zeros((few, out.shape[1]), F32)
    for h in range(rows // few):
        carried += wire[h * few : (h + 1) * few].astype(F32) * count[:, h : h + 1]
    node = jnp.sum(grad_agg, axis=0, keepdims=True) + jnp.sum(carried, axis=0, keepdims=True)

    part_w1 = dot(saved_ref[...], grad_z, FIRST)
    sum_z = jnp.sum(grad_z.astype(F32), axis=0, keepdims=True)
    sum_out = jnp.sum(out.astype(F32), axis=0, keepdims=True)
    quarters = [
        (part_w1[:, :LANES], sum_z[:, :LANES]),
        (part_w1[:, LANES:], sum_z[:, LANES:]),
        (part_w2[:, :LANES], sum_out),
        (part_w2[:, LANES:], node),
    ]

    for step, (wide, thin) in enumerate(quarters):
        rows_ref[step, half:, :LANES] = wide.astype(BF16)
        rows_ref[step, half:, LANES:] = remainders(wide, columns(thin))
        selects, indices = (chosen_ref, index_ref) if step < early else (more_chosen_ref, more_index_ref)
        at = step if step < early else step - early
        both = dot(selects[at], rows_ref[step]).astype(BF16)
        piece_ref[step * block : (step + 1) * block, :] = jnp.where(
            indices[at] >= half, both[:, LANES:], both[:, :LANES]
        )


def local_kernel(lists_ref, recv_ref, wire_ref, agg_ref, total_ref, target_ref, counts_ref):
    rows = wire_ref.shape[0]
    row_index = iota((rows, 1), 0).astype(jnp.int16)
    for tile in range(rows // LANES):
        lists = lists_ref[:, tile * LANES : (tile + 1) * LANES].astype(jnp.int16)
        counts = match(lists[0:1], row_index)
        for k in range(1, lists_ref.shape[0]):
            counts += match(lists[k : k + 1], row_index)
        counts_ref[:, tile * LANES : (tile + 1) * LANES] = counts
    local = dot(wire_ref[...].T, counts_ref[...])
    total_ref[...] = agg_ref[...] + local.T
    target_ref[...] = recv_ref[...]


def chunk_kernel(piece, scale, arrived_ref, share_ref):
    span = piece * LANES
    lane = iota((16, span), 1)
    place = lane - piece * ((lane * ((1 << 16) // piece + 1)) >> 16)
    pick = jnp.where(place == piece - EXTRA + iota((16, span), 0), 1.0, 0.0).astype(BF16)
    sums = jnp.zeros((16, LANES), F32)
    for start in range(0, arrived_ref.shape[0], span):
        sums += dot(pick, arrived_ref[start : start + span, :])
    high, low = sums[0:1], sums[1:2]
    lane = iota(high.shape, 1)
    last = jnp.sum(jnp.where(lane >= LANES - 2, low, 0.0), axis=1, keepdims=True)
    wide = scale * (high + jnp.where(lane >= LANES - 2, 0.0, low))
    thin = jnp.broadcast_to(scale * last, wide.shape)
    pair = jnp.concatenate([wide.astype(BF16), remainders(wide, thin)], axis=0)
    share_ref[...] = jnp.concatenate([pair] * (share_ref.shape[0] // EXTRA), axis=0)


def remote_kernel(recv_ref, arrived_ref, total_ref, x_ref):
    rows = total_ref.shape[0]
    row_index = iota((rows, 1), 0).astype(jnp.int16)
    targets = recv_ref[...].astype(jnp.int16)
    total = total_ref[...]
    for r in range(0, recv_ref.shape[0], 2):
        chosen = jnp.concatenate([match(targets[q : q + 1], row_index) for q in (r, r + 1)], axis=1)
        total += dot(chosen, arrived_ref[r * LANES : (r + 2) * LANES, :])
    x_ref[...] = total.astype(BF16)


def last_kernel(share_ref, w1_ref, b1_ref, w2_ref, b2_ref, node_ref, rows_ref):
    count = share_ref.shape[0]
    half = count // 2
    rows_ref[:count, :] = share_ref[...].astype(F32)
    high = rows_ref[pl.ds(0, half, 2), :]
    low = rows_ref[pl.ds(1, half, 2), :]
    lane = iota(high.shape, 1)
    wide = high + jnp.where(lane >= LANES - 2, 0.0, low)
    w1_ref[:, :LANES] = wide[:LANES]
    w1_ref[:, LANES:] = wide[LANES : 2 * LANES]
    w2_ref[:LANES, :] = wide[2 * LANES : 3 * LANES].T
    w2_ref[LANES:, :] = wide[3 * LANES :].T
    thin = []
    for q in range(4):
        turned = low[q * LANES : (q + 1) * LANES].T
        thin.append(turned[LANES - 2 : LANES - 1] + turned[LANES - 1 :])
    b1_ref[...] = jnp.concatenate(thin[:2], axis=1)
    b2_ref[...] = thin[2]
    node_ref[...] = thin[3]


def call(kernel, outs, scratch=(), limit=24, **cost):
    return pl.pallas_call(
        kernel,
        out_shape=[jax.ShapeDtypeStruct(shape, dtype) for shape, dtype in outs],
        scratch_shapes=list(scratch),
        compiler_params=pltpu.CompilerParams(vmem_limit_bytes=limit << 20),
        cost_estimate=pl.CostEstimate(transcendentals=0, **cost),
    )


def per_device(
    grad_out, agg_saved, hidden_saved, w_one, w_two, local_lists, send_slots, receive_slots
):
    rows, width = grad_out.shape
    hidden = hidden_saved.shape[1]
    nodes, groups, slots = send_slots.shape[2:]
    devices = nodes * groups
    piece = slots + EXTRA
    lists = local_lists.T
    send = jnp.transpose(send_slots[0, 0], (1, 2, 0))
    blocks = devices // LANES
    depth = rows // 2 + LANES
    early = blocks // 2

    def shapes(n):
        return [((n, LANES * piece, depth), BF16), ((n, LANES * piece, LANES), jnp.int16)]

    chosen, index = call(
        functools.partial(choose, rows // 2, range(early)),
        shapes(early),
        flops=2 * 10**9,
        bytes_accessed=early * LANES * piece * depth * 2,
        limit=8,
    )(send)
    pieces, agg, wire = call(
        first_kernel,
        [((devices * piece, width), BF16), ((rows, width), F32), ((rows, width), BF16)],
        [pltpu.VMEM((blocks, depth, 2 * width), BF16)]
        + [pltpu.VMEM(*shape) for shape in shapes(blocks - early)],
        limit=16,
        flops=4 * devices * piece * depth * width,
        bytes_accessed=devices * piece * depth * 2,
    )(chosen, index, send, grad_out, w_two, hidden_saved, w_one, lists, agg_saved)
    recv = jnp.pad(receive_slots[0, 0], ((0, 0), (0, 0), (0, EXTRA)), constant_values=rows)
    total, targets = call(
        local_kernel,
        [((rows, width), F32), ((devices * piece // LANES, LANES), jnp.int32)],
        [pltpu.VMEM((rows, rows), BF16)],
        flops=2 * rows * rows * width,
        bytes_accessed=rows * width * 10,
    )(lists, recv.reshape(-1, LANES), wire, agg)

    def exchange(x, height):
        x = x.reshape(devices, height // 2, 2, width)
        return lax.all_to_all(x, AXES, split_axis=0, concat_axis=0, tiled=True).reshape(-1, width)

    arrived = exchange(pieces, piece)
    (share,) = call(
        functools.partial(chunk_kernel, piece, 1.0 / devices),
        [((devices * EXTRA, width), BF16)],
        flops=2 * 16 * devices * piece * width,
        bytes_accessed=devices * piece * width * 2,
    )(arrived)
    shares = exchange(share, EXTRA)
    (grad_x,) = call(
        remote_kernel,
        [((rows, width), BF16)],
        flops=2 * devices * piece * rows * width,
        bytes_accessed=devices * piece * width * 2,
    )(targets, arrived, total)
    w1, b1, w2, b2, node = call(
        last_kernel,
        [
            ((width, hidden), F32),
            ((1, hidden), F32),
            ((hidden, width), F32),
            ((1, width), F32),
            ((1, width), F32),
        ],
        [pltpu.VMEM((devices * EXTRA + 8, width), F32)],
        flops=0,
        bytes_accessed=devices * EXTRA * width * 2,
    )(shares)
    return grad_x, w1, b1[0], w2, b2[0], node[0]


def solution(mesh):
    placed = (
        P(AXES, None),
        P(AXES, None),
        P(AXES, None),
        P(),
        P(),
        P(AXES, None),
        P("nodes", "grp", None, None, None),
        P("nodes", "grp", None, None, None),
    )
    return jax.shard_map(
        per_device,
        mesh=mesh,
        in_specs=placed,
        out_specs=(P(AXES, None), P(), P(), P(), P(), P()),
        check_vma=False,
    )
```

```python
import functools

import jax
import jax.numpy as jnp
from jax import lax
from jax.experimental import pallas as pl
from jax.experimental.pallas import tpu as pltpu
from jax.sharding import PartitionSpec as P

BF16 = jnp.bfloat16
F32 = jnp.float32
PLAIN = (((1,), (0,)), ((), ()))
LAST = (((1,), (1,)), ((), ()))
FIRST = (((0,), (0,)), ((), ()))
LANES = 128
EXTRA = 2
AXES = ("nodes", "grp")


def dot(a, b, dims=PLAIN):
    return lax.dot_general(a, b, dims, preferred_element_type=F32)


def iota(shape, dim):
    return lax.broadcasted_iota(jnp.int32, shape, dim)


def match(a, b):
    shape = jnp.broadcast_shapes(a.shape, b.shape)
    return jnp.where(a == b, jnp.ones(shape, BF16), jnp.zeros(shape, BF16))


def low_part(value):
    return value - value.astype(BF16).astype(F32)


def columns(row):
    return jnp.broadcast_to(row, (LANES, LANES)).T


def remainders(wide, thin):
    lane = iota(wide.shape, 1)
    low = jnp.where(lane == LANES - 2, thin, low_part(wide))
    return jnp.where(lane == LANES - 1, low_part(thin), low).astype(BF16)


def choose(half, steps, send_ref, chosen_ref, index_ref):
    groups, slots, nodes = send_ref.shape
    block = chosen_ref.shape[1]
    piece = slots + EXTRA
    width = LANES // groups
    row = iota((block, LANES), 0) - (piece * iota((1, LANES), 1) + slots)
    place = jnp.where(row >> 1 == 0, 1.0, 0.0).astype(BF16)
    parts = []
    for g in range(groups):
        parts += [send_ref[g], jnp.full((1, nodes), -1, jnp.int32), jnp.full((1, nodes), 4 * half, jnp.int32)]
    sent = jnp.concatenate(parts, axis=0)
    sent = jnp.concatenate([sent, pltpu.roll(sent, nodes - 1, 1)], axis=0).astype(jnp.int16)
    lane_index = iota((16, half), 1).astype(jnp.int16)
    for i, step in enumerate(steps):
        chosen_ref[i, :, half:] = place
        for n in range(0, width, 2):
            for r in range(0, 2 * groups * piece, 16):
                at = step * width + n
                start = n * groups * piece + r
                index = jnp.broadcast_to(sent[r : r + 16, at : at + 1], (16, LANES))
                index_ref[i, start : start + 16, :] = index
                folded = jnp.where(index >= half, index - half, index)
                for t in range(0, half, LANES):
                    chosen_ref[i, start : start + 16, t : t + LANES] = match(folded, lane_index[:, t : t + LANES])


def first_kernel(
    chosen_ref, index_ref, send_ref, out_ref, w2_ref, hid_ref, w1_ref, lists_ref, saved_ref,
    piece_ref, agg_ref, wire_ref, rows_ref, more_chosen_ref, more_index_ref,
):
    early, block, _ = chosen_ref.shape
    blocks = rows_ref.shape[0]
    groups = send_ref.shape[0]
    rows = out_ref.shape[0]
    half = rows // 2
    out = out_ref[...]
    hidden = hid_ref[...]
    grad_hidden = dot(out, w2_ref[...], LAST)
    part_w2 = dot(out, hidden, FIRST)
    grad_z = jnp.where(hidden > 0, grad_hidden, 0.0).astype(BF16)
    grad_agg = dot(grad_z, w1_ref[...], LAST)
    wire = grad_agg.astype(BF16)
    agg_ref[...] = grad_agg
    wire_ref[...] = wire
    for step in range(blocks):
        rows_ref[step, :half, :LANES] = wire[:half]
        rows_ref[step, :half, LANES:] = wire[half:]
    choose(half, range(early, blocks), send_ref, more_chosen_ref, more_index_ref)

    few = 32
    row_index = iota((few, 1), 0).astype(jnp.int16)
    count = jnp.zeros((few, few), F32)
    for ref in [lists_ref] + [send_ref.at[g] for g in range(groups)]:
        index = ref[...]
        low = (index & (few - 1)).astype(jnp.int16)
        high = (index >> 5).astype(jnp.int16)
        for k in range(index.shape[0]):
            count += dot(match(low[k : k + 1], row_index), match(high[k : k + 1], row_index), LAST)
    carried = jnp.zeros((few, out.shape[1]), F32)
    for h in range(rows // few):
        carried += wire[h * few : (h + 1) * few].astype(F32) * count[:, h : h + 1]
    node = jnp.sum(grad_agg, axis=0, keepdims=True) + jnp.sum(carried, axis=0, keepdims=True)

    part_w1 = dot(saved_ref[...], grad_z, FIRST)
    sum_z = jnp.sum(grad_z.astype(F32), axis=0, keepdims=True)
    sum_out = jnp.sum(out.astype(F32), axis=0, keepdims=True)
    quarters = [
        (part_w1[:, :LANES], sum_z[:, :LANES]),
        (part_w1[:, LANES:], sum_z[:, LANES:]),
        (part_w2[:, :LANES], sum_out),
        (part_w2[:, LANES:], node),
    ]

    for step, (wide, thin) in enumerate(quarters):
        rows_ref[step, half:, :LANES] = wide.astype(BF16)
        rows_ref[step, half:, LANES:] = remainders(wide, columns(thin))
        selects, indices = (chosen_ref, index_ref) if step < early else (more_chosen_ref, more_index_ref)
        at = step if step < early else step - early
        both = dot(selects[at], rows_ref[step]).astype(BF16)
        piece_ref[step * block : (step + 1) * block, :] = jnp.where(
            indices[at] >= half, both[:, LANES:], both[:, :LANES]
        )


def local_kernel(lists_ref, recv_ref, wire_ref, agg_ref, total_ref, target_ref, counts_ref):
    rows = wire_ref.shape[0]
    row_index = iota((rows, 1), 0).astype(jnp.int16)
    for tile in range(rows // LANES):
        lists = lists_ref[:, tile * LANES : (tile + 1) * LANES].astype(jnp.int16)
        counts = match(lists[0:1], row_index)
        for k in range(1, lists_ref.shape[0]):
            counts += match(lists[k : k + 1], row_index)
        counts_ref[:, tile * LANES : (tile + 1) * LANES] = counts
    local = dot(wire_ref[...].T, counts_ref[...])
    total_ref[...] = agg_ref[...] + local.T
    target_ref[...] = recv_ref[...]


def chunk_kernel(piece, scale, arrived_ref, share_ref):
    span = piece * LANES
    lane = iota((16, span), 1)
    place = lane - piece * ((lane * ((1 << 16) // piece + 1)) >> 16)
    pick = jnp.where(place == piece - EXTRA + iota((16, span), 0), 1.0, 0.0).astype(BF16)
    sums = jnp.zeros((16, LANES), F32)
    for start in range(0, arrived_ref.shape[0], span):
        sums += dot(pick, arrived_ref[start : start + span, :])
    high, low = sums[0:1], sums[1:2]
    lane = iota(high.shape, 1)
    last = jnp.sum(jnp.where(lane >= LANES - 2, low, 0.0), axis=1, keepdims=True)
    wide = scale * (high + jnp.where(lane >= LANES - 2, 0.0, low))
    thin = jnp.broadcast_to(scale * last, wide.shape)
    pair = jnp.concatenate([wide.astype(BF16), remainders(wide, thin)], axis=0)
    share_ref[...] = jnp.concatenate([pair] * (share_ref.shape[0] // EXTRA), axis=0)


def remote_kernel(recv_ref, arrived_ref, total_ref, x_ref):
    rows = total_ref.shape[0]
    row_index = iota((rows, 1), 0).astype(jnp.int16)
    targets = recv_ref[...].astype(jnp.int16)
    total = total_ref[...]
    for r in range(0, recv_ref.shape[0], 2):
        chosen = jnp.concatenate([match(targets[q : q + 1], row_index) for q in (r, r + 1)], axis=1)
        total += dot(chosen, arrived_ref[r * LANES : (r + 2) * LANES, :])
    x_ref[...] = total.astype(BF16)


def last_kernel(share_ref, w1_ref, b1_ref, w2_ref, b2_ref, node_ref, rows_ref):
    count = share_ref.shape[0]
    half = count // 2
    rows_ref[:count, :] = share_ref[...].astype(F32)
    high = rows_ref[pl.ds(0, half, 2), :]
    low = rows_ref[pl.ds(1, half, 2), :]
    lane = iota(high.shape, 1)
    wide = high + jnp.where(lane >= LANES - 2, 0.0, low)
    w1_ref[:, :LANES] = wide[:LANES]
    w1_ref[:, LANES:] = wide[LANES : 2 * LANES]
    w2_ref[:LANES, :] = wide[2 * LANES : 3 * LANES].T
    w2_ref[LANES:, :] = wide[3 * LANES :].T
    thin = []
    for q in range(4):
        turned = low[q * LANES : (q + 1) * LANES].T
        thin.append(turned[LANES - 2 : LANES - 1] + turned[LANES - 1 :])
    b1_ref[...] = jnp.concatenate(thin[:2], axis=1)
    b2_ref[...] = thin[2]
    node_ref[...] = thin[3]


def call(kernel, outs, scratch=(), limit=24, **cost):
    return pl.pallas_call(
        kernel,
        out_shape=[jax.ShapeDtypeStruct(shape, dtype) for shape, dtype in outs],
        scratch_shapes=list(scratch),
        compiler_params=pltpu.CompilerParams(vmem_limit_bytes=limit << 20),
        cost_estimate=pl.CostEstimate(transcendentals=0, **cost),
    )


def per_device(
    grad_out, agg_saved, hidden_saved, w_one, w_two, local_lists, send_slots, receive_slots
):
    rows, width = grad_out.shape
    hidden = hidden_saved.shape[1]
    nodes, groups, slots = send_slots.shape[2:]
    devices = nodes * groups
    piece = slots + EXTRA
    lists = local_lists.T
    send = jnp.transpose(send_slots[0, 0], (1, 2, 0))
    blocks = devices // LANES
    depth = rows // 2 + LANES
    early = blocks - blocks // 4

    def shapes(n):
        return [((n, LANES * piece, depth), BF16), ((n, LANES * piece, LANES), jnp.int16)]

    chosen, index = call(
        functools.partial(choose, rows // 2, range(early)),
        shapes(early),
        flops=2 * 10**9,
        bytes_accessed=early * LANES * piece * depth * 2,
        limit=8,
    )(send)
    pieces, agg, wire = call(
        first_kernel,
        [((devices * piece, width), BF16), ((rows, width), F32), ((rows, width), BF16)],
        [pltpu.VMEM((blocks, depth, 2 * width), BF16)]
        + [pltpu.VMEM(*shape) for shape in shapes(blocks - early)],
        limit=16,
        flops=4 * devices * piece * depth * width,
        bytes_accessed=devices * piece * depth * 2,
    )(chosen, index, send, grad_out, w_two, hidden_saved, w_one, lists, agg_saved)
    recv = jnp.pad(receive_slots[0, 0], ((0, 0), (0, 0), (0, EXTRA)), constant_values=rows)
    total, targets = call(
        local_kernel,
        [((rows, width), F32), ((devices * piece // LANES, LANES), jnp.int32)],
        [pltpu.VMEM((rows, rows), BF16)],
        flops=2 * rows * rows * width,
        bytes_accessed=rows * width * 10,
    )(lists, recv.reshape(-1, LANES), wire, agg)

    def exchange(x, height):
        x = x.reshape(devices, height // 2, 2, width)
        return lax.all_to_all(x, AXES, split_axis=0, concat_axis=0, tiled=True).reshape(-1, width)

    arrived = exchange(pieces, piece)
    (share,) = call(
        functools.partial(chunk_kernel, piece, 1.0 / devices),
        [((devices * EXTRA, width), BF16)],
        flops=2 * 16 * devices * piece * width,
        bytes_accessed=devices * piece * width * 2,
    )(arrived)
    shares = exchange(share, EXTRA)
    (grad_x,) = call(
        remote_kernel,
        [((rows, width), BF16)],
        flops=2 * devices * piece * rows * width,
        bytes_accessed=devices * piece * width * 2,
    )(targets, arrived, total)
    w1, b1, w2, b2, node = call(
        last_kernel,
        [
            ((width, hidden), F32),
            ((1, hidden), F32),
            ((hidden, width), F32),
            ((1, width), F32),
            ((1, width), F32),
        ],
        [pltpu.VMEM((devices * EXTRA + 8, width), F32)],
        flops=0,
        bytes_accessed=devices * EXTRA * width * 2,
    )(shares)
    return grad_x, w1, b1[0], w2, b2[0], node[0]


def solution(mesh):
    placed = (
        P(AXES, None),
        P(AXES, None),
        P(AXES, None),
        P(),
        P(),
        P(AXES, None),
        P("nodes", "grp", None, None, None),
        P("nodes", "grp", None, None, None),
    )
    return jax.shard_map(
        per_device,
        mesh=mesh,
        in_specs=placed,
        out_specs=(P(AXES, None), P(), P(), P(), P(), P()),
        check_vma=False,
    )
```

```python
import functools

import jax
import jax.numpy as jnp
from jax import lax
from jax.experimental import pallas as pl
from jax.experimental.pallas import tpu as pltpu
from jax.sharding import PartitionSpec as P

BF16 = jnp.bfloat16
F32 = jnp.float32
PLAIN = (((1,), (0,)), ((), ()))
LAST = (((1,), (1,)), ((), ()))
FIRST = (((0,), (0,)), ((), ()))
LANES = 128
EXTRA = 2
AXES = ("nodes", "grp")


def dot(a, b, dims=PLAIN):
    return lax.dot_general(a, b, dims, preferred_element_type=F32)


def iota(shape, dim):
    return lax.broadcasted_iota(jnp.int32, shape, dim)


def match(a, b):
    shape = jnp.broadcast_shapes(a.shape, b.shape)
    return jnp.where(a == b, jnp.ones(shape, BF16), jnp.zeros(shape, BF16))


def low_part(value):
    return value - value.astype(BF16).astype(F32)


def columns(row):
    return jnp.broadcast_to(row, (LANES, LANES)).T


def remainders(wide, thin):
    lane = iota(wide.shape, 1)
    low = jnp.where(lane == LANES - 2, thin, low_part(wide))
    return jnp.where(lane == LANES - 1, low_part(thin), low).astype(BF16)


def choose(half, steps, send_ref, chosen_ref, index_ref):
    groups, slots, nodes = send_ref.shape
    block = chosen_ref.shape[1]
    piece = slots + EXTRA
    width = LANES // groups
    row = iota((block, LANES), 0) - (piece * iota((1, LANES), 1) + slots)
    place = jnp.where(row >> 1 == 0, 1.0, 0.0).astype(BF16)
    parts = []
    for g in range(groups):
        parts += [send_ref[g], jnp.full((1, nodes), -1, jnp.int32), jnp.full((1, nodes), 4 * half, jnp.int32)]
    sent = jnp.concatenate(parts, axis=0)
    sent = jnp.concatenate([sent, pltpu.roll(sent, nodes - 1, 1)], axis=0).astype(jnp.int16)
    lane_index = iota((16, half), 1).astype(jnp.int16)
    for i, step in enumerate(steps):
        chosen_ref[i, :, half:] = place
        for n in range(0, width, 2):
            for r in range(0, 2 * groups * piece, 16):
                at = step * width + n
                start = n * groups * piece + r
                index = jnp.broadcast_to(sent[r : r + 16, at : at + 1], (16, LANES))
                index_ref[i, start : start + 16, :] = index
                folded = jnp.where(index >= half, index - half, index)
                for t in range(0, half, LANES):
                    chosen_ref[i, start : start + 16, t : t + LANES] = match(folded, lane_index[:, t : t + LANES])


def first_kernel(
    chosen_ref, index_ref, send_ref, out_ref, w2_ref, hid_ref, w1_ref, lists_ref, saved_ref,
    piece_ref, agg_ref, wire_ref, rows_ref, more_chosen_ref, more_index_ref,
):
    early, block, _ = chosen_ref.shape
    blocks = rows_ref.shape[0]
    groups = send_ref.shape[0]
    rows = out_ref.shape[0]
    half = rows // 2
    out = out_ref[...]
    hidden = hid_ref[...]
    grad_hidden = dot(out, w2_ref[...], LAST)
    part_w2 = dot(out, hidden, FIRST)
    grad_z = jnp.where(hidden > 0, grad_hidden, 0.0).astype(BF16)
    grad_agg = dot(grad_z, w1_ref[...], LAST)
    wire = grad_agg.astype(BF16)
    agg_ref[...] = grad_agg
    wire_ref[...] = wire
    for step in range(blocks):
        rows_ref[step, :half, :LANES] = wire[:half]
        rows_ref[step, :half, LANES:] = wire[half:]
    choose(half, range(early, blocks), send_ref, more_chosen_ref, more_index_ref)

    few = 32
    row_index = iota((few, 1), 0).astype(jnp.int16)
    count = jnp.zeros((few, few), F32)
    for ref in [lists_ref] + [send_ref.at[g] for g in range(groups)]:
        index = ref[...]
        low = (index & (few - 1)).astype(jnp.int16)
        high = (index >> 5).astype(jnp.int16)
        for k in range(index.shape[0]):
            count += dot(match(low[k : k + 1], row_index), match(high[k : k + 1], row_index), LAST)
    carried = jnp.zeros((few, out.shape[1]), F32)
    for h in range(rows // few):
        carried += wire[h * few : (h + 1) * few].astype(F32) * count[:, h : h + 1]
    node = jnp.sum(grad_agg, axis=0, keepdims=True) + jnp.sum(carried, axis=0, keepdims=True)

    part_w1 = dot(saved_ref[...], grad_z, FIRST)
    sum_z = jnp.sum(grad_z.astype(F32), axis=0, keepdims=True)
    sum_out = jnp.sum(out.astype(F32), axis=0, keepdims=True)
    quarters = [
        (part_w1[:, :LANES], sum_z[:, :LANES]),
        (part_w1[:, LANES:], sum_z[:, LANES:]),
        (part_w2[:, :LANES], sum_out),
        (part_w2[:, LANES:], node),
    ]

    for step, (wide, thin) in enumerate(quarters):
        rows_ref[step, half:, :LANES] = wide.astype(BF16)
        rows_ref[step, half:, LANES:] = remainders(wide, columns(thin))
        selects, indices = (chosen_ref, index_ref) if step < early else (more_chosen_ref, more_index_ref)
        at = step if step < early else step - early
        both = dot(selects[at], rows_ref[step]).astype(BF16)
        piece_ref[step * block : (step + 1) * block, :] = jnp.where(
            indices[at] >= half, both[:, LANES:], both[:, :LANES]
        )


def chunk_kernel(piece, scale, arrived_ref, share_ref):
    span = piece * LANES
    lane = iota((16, span), 1)
    place = lane - piece * ((lane * ((1 << 16) // piece + 1)) >> 16)
    pick = jnp.where(place == piece - EXTRA + iota((16, span), 0), 1.0, 0.0).astype(BF16)
    sums = jnp.zeros((16, LANES), F32)
    for start in range(0, arrived_ref.shape[0], span):
        sums += dot(pick, arrived_ref[start : start + span, :])
    high, low = sums[0:1], sums[1:2]
    lane = iota(high.shape, 1)
    last = jnp.sum(jnp.where(lane >= LANES - 2, low, 0.0), axis=1, keepdims=True)
    wide = scale * (high + jnp.where(lane >= LANES - 2, 0.0, low))
    thin = jnp.broadcast_to(scale * last, wide.shape)
    pair = jnp.concatenate([wide.astype(BF16), remainders(wide, thin)], axis=0)
    share_ref[...] = jnp.concatenate([pair] * (share_ref.shape[0] // EXTRA), axis=0)


def edges_kernel(lists_ref, recv_ref, wire_ref, agg_ref, arrived_ref, x_ref, counts_ref):
    rows = wire_ref.shape[0]
    row_index = iota((rows, 1), 0).astype(jnp.int16)
    for tile in range(rows // LANES):
        lists = lists_ref[:, tile * LANES : (tile + 1) * LANES].astype(jnp.int16)
        counts = match(lists[0:1], row_index)
        for k in range(1, lists_ref.shape[0]):
            counts += match(lists[k : k + 1], row_index)
        counts_ref[:, tile * LANES : (tile + 1) * LANES] = counts
    total = agg_ref[...] + dot(wire_ref[...].T, counts_ref[...]).T
    targets = recv_ref[...].astype(jnp.int16)
    for r in range(0, recv_ref.shape[0], 2):
        chosen = jnp.concatenate([match(targets[q : q + 1], row_index) for q in (r, r + 1)], axis=1)
        total += dot(chosen, arrived_ref[r * LANES : (r + 2) * LANES, :])
    x_ref[...] = total.astype(BF16)


def last_kernel(share_ref, w1_ref, b1_ref, w2_ref, b2_ref, node_ref, rows_ref):
    count = share_ref.shape[0]
    half = count // 2
    rows_ref[:count, :] = share_ref[...].astype(F32)
    high = rows_ref[pl.ds(0, half, 2), :]
    low = rows_ref[pl.ds(1, half, 2), :]
    lane = iota(high.shape, 1)
    wide = high + jnp.where(lane >= LANES - 2, 0.0, low)
    w1_ref[:, :LANES] = wide[:LANES]
    w1_ref[:, LANES:] = wide[LANES : 2 * LANES]
    w2_ref[:LANES, :] = wide[2 * LANES : 3 * LANES].T
    w2_ref[LANES:, :] = wide[3 * LANES :].T
    thin = []
    for q in range(4):
        turned = low[q * LANES : (q + 1) * LANES].T
        thin.append(turned[LANES - 2 : LANES - 1] + turned[LANES - 1 :])
    b1_ref[...] = jnp.concatenate(thin[:2], axis=1)
    b2_ref[...] = thin[2]
    node_ref[...] = thin[3]


def call(kernel, outs, scratch=(), limit=24, **cost):
    return pl.pallas_call(
        kernel,
        out_shape=[jax.ShapeDtypeStruct(shape, dtype) for shape, dtype in outs],
        scratch_shapes=list(scratch),
        compiler_params=pltpu.CompilerParams(vmem_limit_bytes=limit << 20),
        cost_estimate=pl.CostEstimate(transcendentals=0, **cost),
    )


def per_device(
    grad_out, agg_saved, hidden_saved, w_one, w_two, local_lists, send_slots, receive_slots
):
    rows, width = grad_out.shape
    hidden = hidden_saved.shape[1]
    nodes, groups, slots = send_slots.shape[2:]
    devices = nodes * groups
    piece = slots + EXTRA
    lists = local_lists.T
    send = jnp.transpose(send_slots[0, 0], (1, 2, 0))
    blocks = devices // LANES
    depth = rows // 2 + LANES
    early = blocks - blocks // 4

    def shapes(n):
        return [((n, LANES * piece, depth), BF16), ((n, LANES * piece, LANES), jnp.int16)]

    chosen, index = call(
        functools.partial(choose, rows // 2, range(early)),
        shapes(early),
        flops=2 * 10**9,
        bytes_accessed=early * LANES * piece * depth * 2,
        limit=8,
    )(send)
    pieces, agg, wire = call(
        first_kernel,
        [((devices * piece, width), BF16), ((rows, width), F32), ((rows, width), BF16)],
        [pltpu.VMEM((blocks, depth, 2 * width), BF16)]
        + [pltpu.VMEM(*shape) for shape in shapes(blocks - early)],
        limit=16,
        flops=4 * devices * piece * depth * width,
        bytes_accessed=devices * piece * depth * 2,
    )(chosen, index, send, grad_out, w_two, hidden_saved, w_one, lists, agg_saved)
    recv = jnp.pad(receive_slots[0, 0], ((0, 0), (0, 0), (0, EXTRA)), constant_values=rows)
    def exchange(x, height):
        x = x.reshape(devices, height // 2, 2, width)
        return lax.all_to_all(x, AXES, split_axis=0, concat_axis=0, tiled=True).reshape(-1, width)

    arrived = exchange(pieces, piece)
    (share,) = call(
        functools.partial(chunk_kernel, piece, 1.0 / devices),
        [((devices * EXTRA, width), BF16)],
        flops=2 * 16 * devices * piece * width,
        bytes_accessed=devices * piece * width * 2,
    )(arrived)
    shares = exchange(share, EXTRA)
    (grad_x,) = call(
        edges_kernel,
        [((rows, width), BF16)],
        [pltpu.VMEM((rows, rows), BF16)],
        flops=2 * (devices * piece + rows) * rows * width,
        bytes_accessed=devices * piece * width * 2,
    )(lists, recv.reshape(-1, LANES), wire, agg, arrived)
    w1, b1, w2, b2, node = call(
        last_kernel,
        [
            ((width, hidden), F32),
            ((1, hidden), F32),
            ((hidden, width), F32),
            ((1, width), F32),
            ((1, width), F32),
        ],
        [pltpu.VMEM((devices * EXTRA + 8, width), F32)],
        flops=0,
        bytes_accessed=devices * EXTRA * width * 2,
    )(shares)
    return grad_x, w1, b1[0], w2, b2[0], node[0]


def solution(mesh):
    placed = (
        P(AXES, None),
        P(AXES, None),
        P(AXES, None),
        P(),
        P(),
        P(AXES, None),
        P("nodes", "grp", None, None, None),
        P("nodes", "grp", None, None, None),
    )
    return jax.shard_map(
        per_device,
        mesh=mesh,
        in_specs=placed,
        out_specs=(P(AXES, None), P(), P(), P(), P(), P()),
        check_vma=False,
    )
```

```python
import functools

import jax
import jax.numpy as jnp
from jax import lax
from jax.experimental import pallas as pl
from jax.experimental.pallas import tpu as pltpu
from jax.sharding import PartitionSpec as P

BF16 = jnp.bfloat16
F32 = jnp.float32
PLAIN = (((1,), (0,)), ((), ()))
LAST = (((1,), (1,)), ((), ()))
FIRST = (((0,), (0,)), ((), ()))
LANES = 128
EXTRA = 2
AXES = ("nodes", "grp")


def dot(a, b, dims=PLAIN):
    return lax.dot_general(a, b, dims, preferred_element_type=F32)


def iota(shape, dim):
    return lax.broadcasted_iota(jnp.int32, shape, dim)


def match(a, b):
    shape = jnp.broadcast_shapes(a.shape, b.shape)
    return jnp.where(a == b, jnp.ones(shape, BF16), jnp.zeros(shape, BF16))


def low_part(value):
    return value - value.astype(BF16).astype(F32)


def columns(row):
    return jnp.broadcast_to(row, (LANES, LANES)).T


def remainders(wide, thin):
    lane = iota(wide.shape, 1)
    low = jnp.where(lane == LANES - 2, thin, low_part(wide))
    return jnp.where(lane == LANES - 1, low_part(thin), low).astype(BF16)


def choose(half, steps, send_ref, chosen_ref, index_ref):
    groups, slots, nodes = send_ref.shape
    block = chosen_ref.shape[1]
    piece = slots + EXTRA
    width = LANES // groups
    row = iota((block, LANES), 0) - (piece * iota((1, LANES), 1) + slots)
    place = jnp.where(row >> 1 == 0, 1.0, 0.0).astype(BF16)
    parts = []
    for g in range(groups):
        parts += [send_ref[g], jnp.full((1, nodes), -1, jnp.int32), jnp.full((1, nodes), 4 * half, jnp.int32)]
    sent = jnp.concatenate(parts, axis=0)
    sent = jnp.concatenate([sent, pltpu.roll(sent, nodes - 1, 1)], axis=0).astype(jnp.int16)
    lane_index = iota((16, half), 1).astype(jnp.int16)
    for i, step in enumerate(steps):
        chosen_ref[i, :, half:] = place
        for n in range(0, width, 2):
            for r in range(0, 2 * groups * piece, 16):
                at = step * width + n
                start = n * groups * piece + r
                index = jnp.broadcast_to(sent[r : r + 16, at : at + 1], (16, LANES))
                index_ref[i, start : start + 16, :] = index
                folded = jnp.where(index >= half, index - half, index)
                for t in range(0, half, LANES):
                    chosen_ref[i, start : start + 16, t : t + LANES] = match(folded, lane_index[:, t : t + LANES])


def first_kernel(
    chosen_ref, index_ref, send_ref, out_ref, w2_ref, hid_ref, w1_ref, lists_ref, saved_ref,
    piece_ref, agg_ref, wire_ref, rows_ref, more_chosen_ref, more_index_ref,
):
    early, block, _ = chosen_ref.shape
    blocks = rows_ref.shape[0]
    groups = send_ref.shape[0]
    rows = out_ref.shape[0]
    half = rows // 2
    out = out_ref[...]
    hidden = hid_ref[...]
    grad_hidden = dot(out, w2_ref[...], LAST)
    part_w2 = dot(out, hidden, FIRST)
    grad_z = jnp.where(hidden > 0, grad_hidden, 0.0).astype(BF16)
    grad_agg = dot(grad_z, w1_ref[...], LAST)
    wire = grad_agg.astype(BF16)
    agg_ref[...] = grad_agg
    wire_ref[...] = wire
    for step in range(blocks):
        rows_ref[step, :half, :LANES] = wire[:half]
        rows_ref[step, :half, LANES:] = wire[half:]
    choose(half, range(early, blocks), send_ref, more_chosen_ref, more_index_ref)

    few = 32
    row_index = iota((few, 1), 0).astype(jnp.int16)
    count = jnp.zeros((few, few), F32)
    for index in (lists_ref[...], jnp.concatenate([send_ref[g] for g in range(groups)], axis=1)):
        low = (index & (few - 1)).astype(jnp.int16)
        high = (index >> 5).astype(jnp.int16)
        for k in range(index.shape[0]):
            count += dot(match(low[k : k + 1], row_index), match(high[k : k + 1], row_index), LAST)
    carried = jnp.zeros((few, out.shape[1]), F32)
    for h in range(rows // few):
        carried += wire[h * few : (h + 1) * few].astype(F32) * count[:, h : h + 1]
    node = jnp.sum(grad_agg, axis=0, keepdims=True) + jnp.sum(carried, axis=0, keepdims=True)

    part_w1 = dot(saved_ref[...], grad_z, FIRST)
    sum_z = jnp.sum(grad_z.astype(F32), axis=0, keepdims=True)
    sum_out = jnp.sum(out.astype(F32), axis=0, keepdims=True)
    quarters = [
        (part_w1[:, :LANES], sum_z[:, :LANES]),
        (part_w1[:, LANES:], sum_z[:, LANES:]),
        (part_w2[:, :LANES], sum_out),
        (part_w2[:, LANES:], node),
    ]

    for step, (wide, thin) in enumerate(quarters):
        rows_ref[step, half:, :LANES] = wide.astype(BF16)
        rows_ref[step, half:, LANES:] = remainders(wide, columns(thin))
        selects, indices = (chosen_ref, index_ref) if step < early else (more_chosen_ref, more_index_ref)
        at = step if step < early else step - early
        both = dot(selects[at], rows_ref[step]).astype(BF16)
        piece_ref[step * block : (step + 1) * block, :] = jnp.where(
            indices[at] >= half, both[:, LANES:], both[:, :LANES]
        )


def chunk_kernel(piece, scale, arrived_ref, share_ref):
    span = piece * LANES
    lane = iota((16, span), 1)
    place = lane - piece * ((lane * ((1 << 16) // piece + 1)) >> 16)
    pick = jnp.where(place == piece - EXTRA + iota((16, span), 0), 1.0, 0.0).astype(BF16)
    sums = jnp.zeros((16, LANES), F32)
    for start in range(0, arrived_ref.shape[0], span):
        sums += dot(pick, arrived_ref[start : start + span, :])
    high, low = sums[0:1], sums[1:2]
    lane = iota(high.shape, 1)
    last = jnp.sum(jnp.where(lane >= LANES - 2, low, 0.0), axis=1, keepdims=True)
    wide = scale * (high + jnp.where(lane >= LANES - 2, 0.0, low))
    thin = jnp.broadcast_to(scale * last, wide.shape)
    pair = jnp.concatenate([wide.astype(BF16), remainders(wide, thin)], axis=0)
    share_ref[...] = jnp.concatenate([pair] * (share_ref.shape[0] // EXTRA), axis=0)


def edges_kernel(lists_ref, recv_ref, wire_ref, agg_ref, arrived_ref, x_ref, counts_ref):
    rows = wire_ref.shape[0]
    row_index = iota((rows, 1), 0).astype(jnp.int16)
    for tile in range(rows // LANES):
        lists = lists_ref[:, tile * LANES : (tile + 1) * LANES].astype(jnp.int16)
        counts = match(lists[0:1], row_index)
        for k in range(1, lists_ref.shape[0]):
            counts += match(lists[k : k + 1], row_index)
        counts_ref[:, tile * LANES : (tile + 1) * LANES] = counts
    total = agg_ref[...] + dot(wire_ref[...].T, counts_ref[...]).T
    targets = recv_ref[...].astype(jnp.int16)
    for r in range(0, recv_ref.shape[0], 2):
        chosen = jnp.concatenate([match(targets[q : q + 1], row_index) for q in (r, r + 1)], axis=1)
        total += dot(chosen, arrived_ref[r * LANES : (r + 2) * LANES, :])
    x_ref[...] = total.astype(BF16)


def last_kernel(share_ref, w1_ref, b1_ref, w2_ref, b2_ref, node_ref, rows_ref):
    count = share_ref.shape[0]
    half = count // 2
    rows_ref[:count, :] = share_ref[...].astype(F32)
    high = rows_ref[pl.ds(0, half, 2), :]
    low = rows_ref[pl.ds(1, half, 2), :]
    lane = iota(high.shape, 1)
    wide = high + jnp.where(lane >= LANES - 2, 0.0, low)
    w1_ref[:, :LANES] = wide[:LANES]
    w1_ref[:, LANES:] = wide[LANES : 2 * LANES]
    w2_ref[:LANES, :] = wide[2 * LANES : 3 * LANES].T
    w2_ref[LANES:, :] = wide[3 * LANES :].T
    thin = []
    for q in range(4):
        turned = low[q * LANES : (q + 1) * LANES].T
        thin.append(turned[LANES - 2 : LANES - 1] + turned[LANES - 1 :])
    b1_ref[...] = jnp.concatenate(thin[:2], axis=1)
    b2_ref[...] = thin[2]
    node_ref[...] = thin[3]


def call(kernel, outs, scratch=(), limit=24, **cost):
    return pl.pallas_call(
        kernel,
        out_shape=[jax.ShapeDtypeStruct(shape, dtype) for shape, dtype in outs],
        scratch_shapes=list(scratch),
        compiler_params=pltpu.CompilerParams(vmem_limit_bytes=limit << 20),
        cost_estimate=pl.CostEstimate(transcendentals=0, **cost),
    )


def per_device(
    grad_out, agg_saved, hidden_saved, w_one, w_two, local_lists, send_slots, receive_slots
):
    rows, width = grad_out.shape
    hidden = hidden_saved.shape[1]
    nodes, groups, slots = send_slots.shape[2:]
    devices = nodes * groups
    piece = slots + EXTRA
    lists = local_lists.T
    send = jnp.transpose(send_slots[0, 0], (1, 2, 0))
    blocks = devices // LANES
    depth = rows // 2 + LANES
    early = blocks - blocks // 4

    def shapes(n):
        return [((n, LANES * piece, depth), BF16), ((n, LANES * piece, LANES), jnp.int16)]

    chosen, index = call(
        functools.partial(choose, rows // 2, range(early)),
        shapes(early),
        flops=2 * 10**9,
        bytes_accessed=early * LANES * piece * depth * 2,
        limit=8,
    )(send)
    pieces, agg, wire = call(
        first_kernel,
        [((devices * piece, width), BF16), ((rows, width), F32), ((rows, width), BF16)],
        [pltpu.VMEM((blocks, depth, 2 * width), BF16)]
        + [pltpu.VMEM(*shape) for shape in shapes(blocks - early)],
        limit=16,
        flops=4 * devices * piece * depth * width,
        bytes_accessed=devices * piece * depth * 2,
    )(chosen, index, send, grad_out, w_two, hidden_saved, w_one, lists, agg_saved)
    recv = jnp.pad(receive_slots[0, 0], ((0, 0), (0, 0), (0, EXTRA)), constant_values=rows)
    def exchange(x, height):
        x = x.reshape(devices, height // 2, 2, width)
        return lax.all_to_all(x, AXES, split_axis=0, concat_axis=0, tiled=True).reshape(-1, width)

    arrived = exchange(pieces, piece)
    (share,) = call(
        functools.partial(chunk_kernel, piece, 1.0 / devices),
        [((devices * EXTRA, width), BF16)],
        flops=2 * 16 * devices * piece * width,
        bytes_accessed=devices * piece * width * 2,
    )(arrived)
    shares = exchange(share, EXTRA)
    (grad_x,) = call(
        edges_kernel,
        [((rows, width), BF16)],
        [pltpu.VMEM((rows, rows), BF16)],
        flops=2 * (devices * piece + rows) * rows * width,
        bytes_accessed=devices * piece * width * 2,
    )(lists, recv.reshape(-1, LANES), wire, agg, arrived)
    w1, b1, w2, b2, node = call(
        last_kernel,
        [
            ((width, hidden), F32),
            ((1, hidden), F32),
            ((hidden, width), F32),
            ((1, width), F32),
            ((1, width), F32),
        ],
        [pltpu.VMEM((devices * EXTRA + 8, width), F32)],
        flops=0,
        bytes_accessed=devices * EXTRA * width * 2,
    )(shares)
    return grad_x, w1, b1[0], w2, b2[0], node[0]


def solution(mesh):
    placed = (
        P(AXES, None),
        P(AXES, None),
        P(AXES, None),
        P(),
        P(),
        P(AXES, None),
        P("nodes", "grp", None, None, None),
        P("nodes", "grp", None, None, None),
    )
    return jax.shard_map(
        per_device,
        mesh=mesh,
        in_specs=placed,
        out_specs=(P(AXES, None), P(), P(), P(), P(), P()),
        check_vma=False,
    )
```
